32 devices in a mesh: section: 2 (over x), gx: 2 (over core), gy: 2 (over y), dp: 4 (over z).
Axes of the slice: x: 2, y: 2, z: 4, core: 2. Of those that a mesh axis runs over, the one named last changes fastest.
Arguments:
- x_input: bfloat16 [2, 4, 2048, 640], P(None, 'dp', ('gx', 'gy')), may hold values from -6 to 6
- doc_lengths: int32 [2, 4, 8], P(None, 'dp'), may hold values from 0 to 2048, as said below
- cotangent: bfloat16 [2, 4, 2048, 640], P(None, 'dp', ('gx', 'gy')), may hold values from -6 to 6
- gain_attn: float32 [2, 640], P('section'), may hold values from 0.25 to 1.75
- w_query: bfloat16 [2, 640, 1024], P('section', None, 'gy'), may hold values from -0.25 to 0.25
- w_key: bfloat16 [2, 640, 256], P('section'), may hold values from -0.25 to 0.25
- w_value: bfloat16 [2, 640, 256], P('section'), may hold values from -0.25 to 0.25
- w_out: bfloat16 [2, 1024, 640], P('section', 'gy'), may hold values from -1.5 to 1.5
- gain_ff: float32 [2, 640], P('section'), may hold values from 0.25 to 1.75
- w_gate: bfloat16 [2, 640, 2048], P('section', None, 'gy'), may hold values from -0.25 to 0.25
- w_up: bfloat16 [2, 640, 2048], P('section', None, 'gy'), may hold values from -0.25 to 0.25
- w_down: bfloat16 [2, 2048, 640], P('section', 'gy'), may hold values from -0.125 to 0.125
Outputs:
- hidden_states: bfloat16 [2, 2, 4, 2048, 640], P('section', None, 'dp', ('gx', 'gy'))
- input_grads: bfloat16 [2, 2, 4, 2048, 640], P('section', None, 'dp', ('gx', 'gy'))
- gain_attn_grad: float32 [2, 640], P('section')
- query_grad: float32 [2, 640, 1024], P('section', None, 'gy')
- key_grad: float32 [2, 640, 256], P('section')
- value_grad: float32 [2, 640, 256], P('section')
- out_grad: float32 [2, 1024, 640], P('section', 'gy')
- gain_ff_grad: float32 [2, 640], P('section')
- gate_grad: float32 [2, 640, 2048], P('section', None, 'gy')
- up_grad: float32 [2, 640, 2048], P('section', None, 'gy')
- down_grad: float32 [2, 2048, 640], P('section', 'gy')
The draws below stay inside these ranges and needn't reach their ends.
Inputs may be any that keep to these rules, and one draw needn't show every extreme that they name: `doc_lengths`: each slot's lengths sum to at most 2048; zero lengths occur.
All inputs are finite; a program needn't handle non-finite values.
Results may differ from the reference program's by a relative error of at most 0.028.
Values may be sent and summed in bfloat16 or wider, within the bound.
No kernel may reach another device: no remote copies, remote signals or barrier semaphores. Data moves between devices by JAX's collectives and lax.ppermute only.
A program may use at most 192 MiB of HBM per device.

```python
import math
import jax
import jax.numpy as jnp
from jax import lax

D = 640
HEADS = 4
HD = 256
FF = 2048
WINDOW = 512
SLOT = 2048
MICRO = 2
DOCS = 8
N_DP = 4


def draw_doc_lengths(key, part):
    key = jax.random.fold_in(key, 17)
    used_key, cut_key, full_key = jax.random.split(key, 3)
    used_rows = jax.random.randint(used_key, (MICRO, N_DP), SLOT * 5 // 8, SLOT + 1)
    cut_points = jax.random.randint(cut_key, (MICRO, N_DP, DOCS - 1), 1, SLOT)
    cut_points = jnp.minimum(cut_points, used_rows[:, :, None])
    inside = (cut_points > SLOT // 2 - WINDOW // 2) & (cut_points < SLOT // 2 + WINDOW // 2)
    cut_points = jnp.where(inside, used_rows[:, :, None], cut_points)
    cut_points = jnp.sort(cut_points, axis=-1)
    bounds = jnp.concatenate([jnp.zeros((MICRO, N_DP, 1), jnp.int32), cut_points, used_rows[:, :, None]], axis=-1)
    lengths = bounds[:, :, 1:] - bounds[:, :, :-1]
    full_shard = jax.random.randint(full_key, (), 0, N_DP)
    full_row = jnp.where(jnp.arange(DOCS) == 0, SLOT, 0)
    chosen = (jnp.arange(MICRO)[:, None] == 0) & (jnp.arange(N_DP)[None, :] == full_shard)
    return jnp.where(chosen[:, :, None], full_row[None, None, :], lengths).astype(jnp.int32)


def level_of(stream_key, shape, pieces, smallest, high):
    factor_of = 1.0
    for position, parts in pieces:
        heights = jax.random.uniform(jax.random.fold_in(jax.random.fold_in(stream_key, 6), position), (parts,), jnp.float32, smallest / len(pieces), high / len(pieces))
        factor_of = factor_of * jnp.repeat(jnp.exp(heights), shape[position] // parts).reshape((-1,) + (1,) * (len(shape) - 1 - position))
    return factor_of


def normal_values(rng, dims, width, limit, cuts=(), kind=jnp.bfloat16):
    array = width * jax.random.normal(rng, dims, jnp.float32)
    if cuts:
        array = array * level_of(rng, dims, cuts, -0.22, 0.18)
    return jnp.clip(array, -limit, limit).astype(kind)


def setup_inputs(seed: int = 0) -> dict:
    key_list = jax.random.split(jax.random.key(seed), 13)
    return {
        "x_input": normal_values(key_list[0], (MICRO, N_DP, SLOT, D), 1.0, 6.0, ((1, 4), (2, 4))),
        "doc_lengths": draw_doc_lengths(jax.random.fold_in(key_list[12], 71), 0),
        "cotangent": normal_values(key_list[2], (MICRO, N_DP, SLOT, D), 1.0, 6.0, ((1, 4), (2, 4))),
        "gain_attn": jnp.clip(1.0 + 0.15 * jax.random.normal(key_list[3], (2, D), jnp.float32), 0.25, 1.75),
        "w_query": normal_values(key_list[4], (2, D, HEADS * HD), D ** -0.5, 0.25, ((0, 2), (2, 2))),
        "w_key": normal_values(key_list[5], (2, D, HD), D ** -0.5, 0.25, ((0, 2),)),
        "w_value": normal_values(key_list[6], (2, D, HD), D ** -0.5, 0.25, ((0, 2),)),
        "w_out": normal_values(key_list[7], (2, HEADS * HD, D), (HEADS * HD // 64) ** -0.5, 1.5, ((0, 2), (1, 2))),
        "gain_ff": jnp.clip(1.0 + 0.15 * jax.random.normal(key_list[8], (2, D), jnp.float32), 0.25, 1.75),
        "w_gate": normal_values(key_list[9], (2, D, FF), D ** -0.5, 0.25, ((0, 2), (2, 2))),
        "w_up": normal_values(key_list[10], (2, D, FF), D ** -0.5, 0.25, ((0, 2), (2, 2))),
        "w_down": normal_values(key_list[11], (2, FF, D), FF ** -0.5, 0.125, ((0, 2), (1, 2))),
    }


@jax.custom_vjp
def low(v):
    return lax.optimization_barrier(v.astype(jnp.bfloat16)).astype(jnp.float32)

@jax.custom_vjp
def low_back(v):
    return v

def low_keep(v):
    return (low(v), None)

def low_pass(kept, grad):
    return (grad,)

def back_keep(v):
    return (v, None)

def back_low(kept, grad):
    return (low(grad),)
low.defvjp(low_keep, low_pass)
low_back.defvjp(back_keep, back_low)

def product(a, b):
    return jnp.dot(a, b, precision=lax.Precision.HIGHEST, preferred_element_type=jnp.float32)

def rms_scale(value, gain):
    return value * lax.rsqrt(lax.optimization_barrier(jnp.mean(value * value, axis=-1, keepdims=True)) + 1e-06) * gain

def rotate(value, cosine_part, sine_part):
    half_width = value.shape[-1] // 2
    first_half = value[..., :half_width]
    second_half = value[..., half_width:]
    return jnp.concatenate([first_half * cosine_part - second_half * sine_part, second_half * cosine_part + first_half * sine_part], axis=-1)

def doc_layout(lengths, slot_rows):
    doc_count = lengths.shape[0]
    doc_ends = jnp.cumsum(lengths)
    starts = doc_ends - lengths
    row_place = jnp.arange(slot_rows, dtype=jnp.int32)
    doc_number = lax.optimization_barrier(jnp.sum((row_place[:, None] >= doc_ends[None, :]).astype(jnp.int32), axis=1))
    valid_rows = doc_number < doc_count
    doc_begin = lax.optimization_barrier(jnp.sum(jnp.where(doc_number[:, None] == jnp.arange(doc_count, dtype=jnp.int32)[None, :], starts[None, :], 0), axis=1))
    where_in = jnp.where(valid_rows, row_place - doc_begin, 0)
    segment = jnp.where(valid_rows, doc_number, doc_count + row_place)
    return (segment, where_in, valid_rows)

def rope_tables(where_in):
    half_width = HD // 2
    frequency = jnp.exp(jnp.arange(half_width, dtype=jnp.float32) * (-2.0 * math.log(10000.0) / HD))
    angles = where_in.astype(jnp.float32)[:, None] * frequency[None, :]
    return (jnp.cos(angles), jnp.sin(angles))

def attention(queries, key_rows, value_rows, segment):
    slot_rows = queries.shape[0]
    block_rows = min(512, slot_rows)
    pad_keys = jnp.concatenate([jnp.zeros((WINDOW, HD), jnp.float32), key_rows], axis=0)
    pad_values = jnp.concatenate([jnp.zeros((WINDOW, HD), jnp.float32), value_rows], axis=0)
    pad_segment = jnp.concatenate([jnp.full((WINDOW,), -1, jnp.int32), segment])

    def one_block(offset):
        q_block = lax.dynamic_slice_in_dim(queries, offset, block_rows, 0)
        k_block = lax.dynamic_slice_in_dim(pad_keys, offset, WINDOW + block_rows, 0)
        v_block = lax.dynamic_slice_in_dim(pad_values, offset, WINDOW + block_rows, 0)
        seg_query = lax.dynamic_slice_in_dim(segment, offset, block_rows, 0)
        seg_key = lax.dynamic_slice_in_dim(pad_segment, offset, WINDOW + block_rows, 0)
        distance = jnp.arange(block_rows, dtype=jnp.int32)[:, None] + WINDOW - jnp.arange(WINDOW + block_rows, dtype=jnp.int32)[None, :]
        allowed = (distance >= 0) & (distance < WINDOW) & (seg_query[:, None] == seg_key[None, :])
        scores = low_back(jnp.einsum('qhd,kd->hqk', q_block, k_block, precision=lax.Precision.HIGHEST))
        scores = jnp.where(allowed[None], scores, -1e+30)
        row_max = lax.optimization_barrier(jnp.max(scores, axis=-1, keepdims=True))
        weights = jnp.exp(scores - row_max)
        probability = low(weights / lax.optimization_barrier(jnp.sum(weights, axis=-1, keepdims=True)))
        return low(low_back(jnp.einsum('hqk,kd->qhd', probability, v_block, precision=lax.Precision.HIGHEST)))
    offsets = jnp.arange(slot_rows // block_rows, dtype=jnp.int32) * block_rows
    mixed_heads = lax.map(jax.checkpoint(one_block), offsets)
    return mixed_heads.reshape(slot_rows, -1)

def layer_apply(inputs, lengths, weights):
    gain_attn, w_query, w_key, w_value, w_out, gain_ff, w_gate, w_up, w_down = weights
    slot_rows = inputs.shape[0]
    segment, where_in, valid_rows = doc_layout(lengths, slot_rows)
    cosine_part, sine_part = rope_tables(where_in)
    normed = low(rms_scale(inputs, gain_attn))
    q_raw = low_back(product(normed, w_query)).reshape(slot_rows, HEADS, HD)
    queries = low(rotate(q_raw, cosine_part[:, None, :], sine_part[:, None, :]) * HD ** (-0.5))
    key_rows = low(rotate(low_back(product(normed, w_key)), cosine_part, sine_part))
    value_rows = low(low_back(product(normed, w_value)))
    mixed_heads = attention(queries, key_rows, value_rows, segment)
    hidden = inputs + low_back(product(mixed_heads, w_out))
    normed_ff = low(rms_scale(hidden, gain_ff))
    gate_value = low_back(product(normed_ff, w_gate))
    up_value = low_back(product(normed_ff, w_up))
    activated = low(jax.nn.gelu(gate_value, approximate=True) * up_value)
    return hidden + low_back(product(activated, w_down))

def reference(x_input, doc_lengths, cotangent, gain_attn, w_query, w_key, w_value, w_out, gain_ff, w_gate, w_up, w_down):
    stacks = tuple((a.astype(jnp.float32) for a in (gain_attn, w_query, w_key, w_value, w_out, gain_ff, w_gate, w_up, w_down)))
    layer_zero = tuple((a[0] for a in stacks))
    layer_one = tuple((a[1] for a in stacks))
    inputs = x_input.astype(jnp.float32).reshape(MICRO * N_DP, SLOT, D)
    cotangents = cotangent.astype(jnp.float32).reshape(MICRO * N_DP, SLOT, D)
    lengths_all = doc_lengths.reshape(MICRO * N_DP, DOCS)
    zero_grads = jax.tree.map(jnp.zeros_like, (layer_zero, layer_one))

    def slot_step(summed, slot_item):
        inputs_here, lengths, cot_here = slot_item
        valid_rows = doc_layout(lengths, SLOT)[2]
        middle, back_zero = jax.vjp(lambda v, w: layer_apply(v, lengths, w), inputs_here, layer_zero)
        middle_low = middle.astype(jnp.bfloat16)
        final_out, back_one = jax.vjp(lambda v, w: layer_apply(v, lengths, w), middle_low.astype(jnp.float32), layer_one)
        grad_middle, grads_one = back_one(cot_here * valid_rows[:, None].astype(jnp.float32))
        grad_middle_low = grad_middle.astype(jnp.bfloat16)
        grad_input, grads_zero = back_zero(grad_middle_low.astype(jnp.float32))
        summed = jax.tree.map(jnp.add, summed, (grads_zero, grads_one))
        return (summed, (middle_low, final_out.astype(jnp.bfloat16), grad_input.astype(jnp.bfloat16), grad_middle_low))
    summed, (middles, finals, grad_inputs, grad_middles) = lax.scan(slot_step, zero_grads, (inputs, lengths_all, cotangents))
    hidden_states = jnp.stack([middles, finals]).reshape(2, MICRO, N_DP, SLOT, D)
    input_grads = jnp.stack([grad_inputs, grad_middles]).reshape(2, MICRO, N_DP, SLOT, D)
    grads = tuple((jnp.stack([summed[0][k], summed[1][k]]) / N_DP for k in range(9)))
    return (hidden_states, input_grads, grads[0], grads[1], grads[2], grads[3], grads[4], grads[5], grads[6], grads[7], grads[8])
```

```python
import math

import jax
import jax.numpy as jnp
from jax import lax
from jax.sharding import PartitionSpec as P

HD = 256
WINDOW = 512
F32 = jnp.float32
BF16 = jnp.bfloat16


def swap(value, axis):
    return lax.ppermute(value, axis, [(0, 1), (1, 0)])


def mm(a, b):
    return jnp.dot(a, b, preferred_element_type=F32)


def mm_t(a, b):
    return lax.dot_general(a, b, (((1,), (1,)), ((), ())), preferred_element_type=F32)


def t_mm(a, b):
    return lax.dot_general(a, b, (((0,), (0,)), ((), ())), preferred_element_type=F32)


def inverse_rms(value):
    return lax.rsqrt(jnp.mean(value * value, axis=-1, keepdims=True) + 1e-06)


def norm_back(value, gain, grad):
    s = inverse_rms(value)
    scaled = grad * gain
    to_value = s * scaled - value * (s * s * s) * jnp.mean(value * scaled, axis=-1, keepdims=True)
    return to_value, jnp.sum(grad * value * s, axis=0)


def rotate(value, cos, sin):
    half = value.shape[-1] // 2
    a, b = value[..., :half], value[..., half:]
    return jnp.concatenate([a * cos - b * sin, b * cos + a * sin], axis=-1)


def unrotate(value, cos, sin):
    half = value.shape[-1] // 2
    c, e = value[..., :half], value[..., half:]
    return jnp.concatenate([c * cos + e * sin, e * cos - c * sin], axis=-1)


def gelu_parts(v):
    c = math.sqrt(2.0 / math.pi)
    t = jnp.tanh(c * (v + 0.044715 * v * v * v))
    value = 0.5 * v * (1.0 + t)
    slope = 0.5 * (1.0 + t) + 0.5 * v * (1.0 - t * t) * (c * (1.0 + 3 * 0.044715 * v * v))
    return value, slope


def layout(lengths, rows):
    docs = lengths.shape[0]
    ends = jnp.cumsum(lengths)
    number = jnp.sum((rows[:, None] >= ends[None, :]).astype(jnp.int32), axis=1)
    valid = number < docs
    begin = jnp.sum(
        jnp.where(number[:, None] == jnp.arange(docs)[None, :], (ends - lengths)[None, :], 0), axis=1
    )
    place = jnp.where(valid, rows - begin, 0)
    segment = jnp.where(rows < 0, -1, jnp.where(valid, number, docs + rows))
    return segment, place, valid


def spread(shard, axis, section):
    half = shard.shape[axis] // 2
    mine = lax.dynamic_slice_in_dim(shard, lax.axis_index("gx") * half, half, axis)
    received = swap(mine, "section")
    layers = []
    for layer in range(2):
        own = jnp.where(section == layer, mine, received)
        beside = swap(own, "gy")
        other = swap(jnp.stack([own, beside]), "gx")
        layers.append([own, beside, other[0], other[1]])
    return layers


def spread_shared(shard, section):
    half = shard.shape[0] // 2
    gx = lax.axis_index("gx")
    mine = lax.dynamic_slice_in_dim(shard, gx * half, half, 0)
    received = swap(mine, "section")
    other = swap(received, "gx")
    low, high = jnp.where(gx == 0, received, other), jnp.where(gx == 0, other, received)
    whole = jnp.concatenate([low, high])
    return [jnp.where(section == layer, shard, whole) for layer in range(2)]


def from_before(value):
    return lax.ppermute(value, ("gx", "gy"), [(0, 1), (1, 2), (2, 3)])


def to_before(value):
    return lax.ppermute(value, ("gx", "gy"), [(1, 0), (2, 1), (3, 2)])


def attend(queries, keys, values, allowed):
    heads, rows, _ = queries.shape
    scores = mm_t(queries.reshape(heads * rows, HD), keys).reshape(heads, rows, -1)
    scores = jnp.where(allowed[None], scores, -1e30)
    top = jnp.max(scores, axis=-1, keepdims=True)
    weights = jnp.exp(scores - top)
    total = jnp.sum(weights, axis=-1, keepdims=True)
    probs = (weights / total).astype(BF16)
    mixed = mm(probs.reshape(heads * rows, -1), values).astype(BF16)
    return mixed.reshape(heads, rows, HD), top + jnp.log(total)


def attend_back(grad_mixed, queries, keys, values, log_total, allowed):
    heads, rows, _ = queries.shape
    flat_q = queries.reshape(heads * rows, HD)
    flat_g = grad_mixed.reshape(heads * rows, HD)
    scores = mm_t(flat_q, keys).reshape(heads, rows, -1)
    probs = jnp.exp(jnp.where(allowed[None], scores, -1e30) - log_total)
    grad_probs = mm_t(flat_g, values).reshape(heads, rows, -1)
    inner = jnp.sum(probs * grad_probs, axis=-1, keepdims=True)
    grad_scores = (probs * (grad_probs - inner)).astype(BF16).reshape(heads * rows, -1)
    probs_low = probs.astype(BF16).reshape(heads * rows, -1)
    grad_queries = mm(grad_scores, keys).reshape(heads, rows, HD)
    return grad_queries, t_mm(grad_scores, flat_q), t_mm(probs_low, flat_g)


def forward_layer(x, w, place):
    cos, sin, allowed = place
    normed = (x * inverse_rms(x) * w["gain_attn"]).astype(BF16)
    keys = rotate(mm(normed, w["key"]), cos, sin).astype(BF16)
    values = mm(normed, w["value"]).astype(BF16)
    before = from_before(jnp.concatenate([keys, values], axis=1))
    queries = jnp.stack(
        [(rotate(mm(normed, p), cos, sin) * HD**-0.5).astype(BF16) for p in w["query"]]
    )
    keys = jnp.concatenate([before[:, :HD], keys])
    values = jnp.concatenate([before[:, HD:], values])
    mixed, log_total = attend(queries, keys, values, allowed)
    hidden = x
    for j, p in enumerate(w["out"]):
        hidden = hidden + mm(mixed[j], p)
    normed_ff = (hidden * inverse_rms(hidden) * w["gain_ff"]).astype(BF16)
    out = hidden
    gates, ups, acts = [], [], []
    for p_gate, p_up, p_down in zip(w["gate"], w["up"], w["down"]):
        gate, up = mm(normed_ff, p_gate), mm(normed_ff, p_up)
        act = (jax.nn.gelu(gate, approximate=True) * up).astype(BF16)
        out = out + mm(act, p_down)
        gates.append(gate)
        ups.append(up)
        acts.append(act)
    kept = (x, normed, queries, keys, values, mixed, log_total, hidden, normed_ff, gates, ups, acts)
    return out, kept


def backward_layer(grad_out, kept, w, place):
    cos, sin, allowed = place
    x, normed, queries, keys, values, mixed, log_total, hidden, normed_ff, gates, ups, acts = kept
    grads = {"gate": [], "up": [], "down": []}
    g_ff = grad_out.astype(BF16)
    grad_normed = 0.0
    for j in range(4):
        d_act = mm_t(g_ff, w["down"][j])
        value, slope = gelu_parts(gates[j])
        d_gate = (d_act * ups[j] * slope).astype(BF16)
        d_up = (d_act * value).astype(BF16)
        grad_normed = grad_normed + mm_t(d_gate, w["gate"][j]) + mm_t(d_up, w["up"][j])
        grads["down"].append(t_mm(acts[j], g_ff))
        grads["gate"].append(t_mm(normed_ff, d_gate))
        grads["up"].append(t_mm(normed_ff, d_up))
    to_hidden, gain_ff = norm_back(hidden, w["gain_ff"], grad_normed)
    grad_hidden = grad_out + to_hidden
    g_attn = grad_hidden.astype(BF16)
    grads["out"] = [t_mm(mixed[j], g_attn) for j in range(4)]
    grad_mixed = jnp.stack([mm_t(g_attn, p).astype(BF16) for p in w["out"]])
    d_queries, d_keys, d_values = attend_back(
        grad_mixed, queries, keys, values, log_total, allowed
    )
    d_both = jnp.concatenate([d_keys, d_values], axis=1)
    behind = to_before(d_both[:WINDOW].astype(BF16))
    grad_normed = 0.0
    grads["query"] = []
    for j in range(4):
        d_q = (unrotate(d_queries[j], cos, sin) * HD**-0.5).astype(BF16)
        grads["query"].append(t_mm(normed, d_q))
        grad_normed = grad_normed + mm_t(d_q, w["query"][j])
    d_both = d_both[WINDOW:] + behind.astype(F32)
    d_k = unrotate(d_both[:, :HD], cos, sin).astype(BF16)
    d_v = d_both[:, HD:].astype(BF16)
    grad_normed = grad_normed + mm_t(d_k, w["key"]) + mm_t(d_v, w["value"])
    grads["shared"] = t_mm(jnp.concatenate([d_k, d_v], axis=1), normed)
    to_x, gain_attn = norm_back(x, w["gain_attn"], grad_normed)
    grads["gains"] = jnp.stack([gain_attn, gain_ff])
    return grad_hidden + to_x, grads


def reduce_pieces(pieces, section, layer):
    pieces = [p.astype(BF16) for p in pieces]
    got = swap(jnp.stack([pieces[2], pieces[3]]), "gx")
    near = pieces[0] + got[0]
    far = pieces[1] + got[1]
    near = near + swap(far, "gy")
    half = near.shape[0] // 2
    keep = lax.dynamic_slice_in_dim(near, section * half, half, 0)
    send = lax.dynamic_slice_in_dim(near, (1 - section) * half, half, 0)
    total = lax.psum(keep + swap(send, "section"), "dp")
    return total, lax.ppermute(total, "section", [(1 - layer, layer)])


def joined(parts, section):
    (own_0, got_0), (own_1, got_1) = parts
    own, got = jnp.where(section == 0, own_0, own_1), jnp.where(section == 0, got_0, got_1)
    return jnp.where(section == 0, jnp.concatenate([own, got]), jnp.concatenate([got, own]))


def both_cores(piece, axis, scale):
    other = swap(piece, "gx")
    first = lax.axis_index("gx") == 0
    low, high = jnp.where(first, piece, other), jnp.where(first, other, piece)
    return jnp.concatenate([low, high], axis=axis).astype(F32) * scale


def local(
    x_input,
    doc_lengths,
    cotangent,
    gain_attn,
    w_query,
    w_key,
    w_value,
    w_out,
    gain_ff,
    w_gate,
    w_up,
    w_down,
):
    section = lax.axis_index("section")
    gx, gy = lax.axis_index("gx"), lax.axis_index("gy")
    own_rows = x_input.shape[2]
    scale = 1.0 / lax.axis_size("dp")

    weights = [{}, {}]

    def put(name, layers):
        for layer in range(2):
            weights[layer][name] = layers[layer]

    gains = jnp.concatenate([gain_attn, gain_ff])
    other_gains = swap(gains, "section")
    for layer in range(2):
        here = jnp.where(section == layer, gains, other_gains)
        weights[layer]["gain_attn"], weights[layer]["gain_ff"] = here[:1], here[1:]
    put("key", spread_shared(w_key[0], section))
    put("value", spread_shared(w_value[0], section))
    put("query", spread(w_query[0], 1, section))
    put("out", spread(w_out[0], 0, section))
    put("gate", spread(w_gate[0], 1, section))
    put("up", spread(w_up[0], 1, section))
    put("down", spread(w_down[0], 0, section))

    lengths = lax.dynamic_index_in_dim(doc_lengths[:, 0], section, 0, keepdims=False)
    x = lax.dynamic_index_in_dim(x_input[:, 0], section, 0, keepdims=False).astype(F32)
    cot = lax.dynamic_index_in_dim(cotangent[:, 0], section, 0, keepdims=False).astype(F32)
    start = (gx * lax.axis_size("gy") + gy) * own_rows
    rows = start - WINDOW + jnp.arange(WINDOW + own_rows, dtype=jnp.int32)
    segment, place, valid = layout(lengths, rows)
    frequency = jnp.exp(jnp.arange(HD // 2, dtype=F32) * (-2.0 * math.log(10000.0) / HD))
    angles = place[WINDOW:].astype(F32)[:, None] * frequency[None, :]
    distance = rows[WINDOW:, None] - rows[None, :]
    allowed = (
        (distance >= 0) & (distance < WINDOW) & (segment[WINDOW:, None] == segment[None, :])
    )
    where = (jnp.cos(angles), jnp.sin(angles), allowed)

    out_0, kept_0 = forward_layer(x, weights[0], where)
    out_0 = out_0.astype(BF16)
    out_1, kept_1 = forward_layer(out_0.astype(F32), weights[1], where)
    out_1 = out_1.astype(BF16)
    states = jnp.where(section == 0, out_0, out_1)
    other_states = swap(jnp.where(section == 0, out_1, out_0), "section")

    grad_1, grads_1 = backward_layer(
        cot * valid[WINDOW:, None].astype(F32), kept_1, weights[1], where
    )
    grad_1 = grad_1.astype(BF16)
    grad_0, grads_0 = backward_layer(grad_1.astype(F32), kept_0, weights[0], where)
    grad_0 = grad_0.astype(BF16)
    in_grads = jnp.where(section == 0, grad_0, grad_1)
    other_grads = swap(jnp.where(section == 0, grad_1, grad_0), "section")

    def by_micro(own, other):
        first = section == 0
        return jnp.stack([jnp.where(first, own, other), jnp.where(first, other, own)])[
            None, :, None
        ]

    def summed(name):
        return joined(
            [reduce_pieces(grads[name], section, i) for i, grads in enumerate((grads_0, grads_1))],
            section,
        )

    def shared_pieces(grads):
        count = grads["shared"].shape[0] // 4
        parts = [grads["shared"][j * count : (j + 1) * count] for j in range(4)]
        index = 2 * gx + gy
        stacked = jnp.stack(parts)
        return [
            lax.dynamic_index_in_dim(stacked, jnp.bitwise_xor(index, flip), 0, keepdims=False)
            for flip in (0, 1, 2, 3)
        ]

    down = summed("down")
    gate = summed("gate")
    up = summed("up")
    out = summed("out")
    query = summed("query")
    shared = joined(
        [reduce_pieces(shared_pieces(g), section, i) for i, g in enumerate((grads_0, grads_1))],
        section,
    )
    shared = lax.all_gather(shared, ("gx", "gy"), axis=0, tiled=True).astype(F32).T * scale
    gain_sums = lax.psum(
        jnp.stack([grads_0["gains"], grads_1["gains"]]), ("section", "gx", "gy", "dp")
    )
    gain_sums = jnp.where(section == 0, gain_sums[0], gain_sums[1]) * scale

    return (
        by_micro(states, other_states),
        by_micro(in_grads, other_grads),
        gain_sums[:1],
        both_cores(query, 1, scale)[None],
        shared[None, :, :HD],
        shared[None, :, HD:],
        both_cores(out, 0, scale)[None],
        gain_sums[1:],
        both_cores(gate, 1, scale)[None],
        both_cores(up, 1, scale)[None],
        both_cores(down, 0, scale)[None],
    )


def solution(mesh):
    rows = P(None, "dp", ("gx", "gy"), None)
    columns = P("section", None, "gy")
    depth = P("section", "gy", None)
    whole = P("section", None, None)
    gain = P("section", None)
    by_layer = P("section", None, "dp", ("gx", "gy"), None)
    return jax.shard_map(
        local,
        mesh=mesh,
        in_specs=(
            rows,
            P(None, "dp", None),
            rows,
            gain,
            columns,
            whole,
            whole,
            depth,
            gain,
            columns,
            columns,
            depth,
        ),
        out_specs=(
            by_layer,
            by_layer,
            gain,
            columns,
            whole,
            whole,
            depth,
            gain,
            columns,
            columns,
            depth,
        ),
        check_vma=False,
    )
```

```python
import math

import jax
import jax.numpy as jnp
from jax import lax
from jax.sharding import PartitionSpec as P

HD = 256
WINDOW = 512
GAIN_ROWS = 32
F32 = jnp.float32
BF16 = jnp.bfloat16


def swap(value, axis):
    return lax.ppermute(value, axis, [(0, 1), (1, 0)])


def mm(a, b):
    return jnp.dot(a, b, preferred_element_type=F32)


def mm_t(a, b):
    return lax.dot_general(a, b, (((1,), (1,)), ((), ())), preferred_element_type=F32)


def t_mm(a, b):
    return lax.dot_general(a, b, (((0,), (0,)), ((), ())), preferred_element_type=F32)


def inverse_rms(value):
    return lax.rsqrt(jnp.mean(value * value, axis=-1, keepdims=True) + 1e-06)


def norm_back(value, gain, grad):
    s = inverse_rms(value)
    scaled = grad * gain
    to_value = s * scaled - value * (s * s * s) * jnp.mean(value * scaled, axis=-1, keepdims=True)
    return to_value, jnp.sum(grad * value * s, axis=0)


def rotate(value, cos, sin):
    half = value.shape[-1] // 2
    a, b = value[..., :half], value[..., half:]
    return jnp.concatenate([a * cos - b * sin, b * cos + a * sin], axis=-1)


def unrotate(value, cos, sin):
    half = value.shape[-1] // 2
    c, e = value[..., :half], value[..., half:]
    return jnp.concatenate([c * cos + e * sin, e * cos - c * sin], axis=-1)


def gelu_parts(v):
    c = math.sqrt(2.0 / math.pi)
    t = jnp.tanh(c * (v + 0.044715 * v * v * v))
    value = 0.5 * v * (1.0 + t)
    slope = 0.5 * (1.0 + t) + 0.5 * v * (1.0 - t * t) * (c * (1.0 + 3 * 0.044715 * v * v))
    return value, slope


def layout(lengths, rows):
    docs = lengths.shape[0]
    ends = jnp.cumsum(lengths)
    number = jnp.sum((rows[:, None] >= ends[None, :]).astype(jnp.int32), axis=1)
    valid = number < docs
    begin = jnp.sum(
        jnp.where(number[:, None] == jnp.arange(docs)[None, :], (ends - lengths)[None, :], 0), axis=1
    )
    place = jnp.where(valid, rows - begin, 0)
    segment = jnp.where(rows < 0, -1, jnp.where(valid, number, docs + rows))
    return segment, place, valid


def pick(flag, a, b):
    return jnp.where(flag, a, b)


def gather_weights(w_query, w_key, w_value, w_out, w_gate, w_up, w_down, section):
    gx = lax.axis_index("gx")

    def half(w, axis):
        size = w.shape[axis] // 2
        return lax.dynamic_slice_in_dim(w, gx * size, size, axis)

    def two_layers(mine, received):
        return [pick(section == layer, mine, received) for layer in range(2)]

    heads, hidden = w_query.shape[1] // 2, w_gate.shape[1] // 2
    first_own = jnp.concatenate([half(w_query, 1), half(w_key, 1), half(w_value, 1)], axis=1)
    out_own = half(w_out, 0)
    wide_own = jnp.concatenate([half(w_gate, 1), half(w_up, 1)], axis=1)
    down_own = half(w_down, 0)
    first_got = swap(first_own, "section")
    down_beside = swap(down_own, "gy")
    out_got = swap(out_own, "section")
    wide_got = swap(wide_own, "section")
    down_own = jnp.concatenate([down_own, down_beside])
    down_got = swap(down_own, "section")

    shared_got = first_got[:, heads:]
    shared_other = swap(shared_got, "gx")
    low, high = pick(gx == 0, shared_got, shared_other), pick(gx == 0, shared_other, shared_got)
    part = low.shape[1] // 2
    key_got = jnp.concatenate([low[:, :part], high[:, :part]], axis=1)
    value_got = jnp.concatenate([low[:, part:], high[:, part:]], axis=1)
    keys, values = two_layers(w_key, key_got), two_layers(w_value, value_got)

    queries = two_layers(first_own[:, :heads], first_got[:, :heads])
    outs = two_layers(out_own, out_got)
    wides = two_layers(wide_own, wide_got)
    downs = two_layers(down_own, down_got)
    layers = []
    for layer in range(2):
        query, out, wide, down = queries[layer], outs[layer], wides[layer], downs[layer]
        query_beside, out_beside, wide_beside = swap(query, "gy"), swap(out, "gy"), swap(wide, "gy")
        wide_pieces = [wide, wide_beside, swap(wide, "gx"), swap(wide_beside, "gx")]
        down_other = swap(down, "gx")
        layers.append(
            {
                "query": [query, query_beside, swap(query, "gx"), swap(query_beside, "gx")],
                "out": [out, out_beside, swap(out, "gx"), swap(out_beside, "gx")],
                "gate": [w[:, :hidden] for w in wide_pieces],
                "up": [w[:, hidden:] for w in wide_pieces],
                "down": [down[:hidden], down[hidden:], down_other[:hidden], down_other[hidden:]],
                "key": keys[layer],
                "value": values[layer],
            }
        )
    return layers


def from_before(value):
    return lax.ppermute(value, ("gx", "gy"), [(0, 1), (1, 2), (2, 3)])


def to_before(value):
    return lax.ppermute(value, ("gx", "gy"), [(1, 0), (2, 1), (3, 2)])


def attend(queries, keys, values, allowed):
    heads, rows, _ = queries.shape
    scores = mm_t(queries.reshape(heads * rows, HD), keys).reshape(heads, rows, -1)
    scores = jnp.where(allowed[None], scores, -1e30)
    top = jnp.max(scores, axis=-1, keepdims=True)
    weights = jnp.exp(scores - top)
    total = jnp.sum(weights, axis=-1, keepdims=True)
    probs = (weights / total).astype(BF16)
    mixed = mm(probs.reshape(heads * rows, -1), values).astype(BF16)
    return mixed.reshape(heads, rows, HD), top + jnp.log(total)


def attend_back(grad_mixed, queries, keys, values, log_total, allowed):
    heads, rows, _ = queries.shape
    flat_q = queries.reshape(heads * rows, HD)
    flat_g = grad_mixed.reshape(heads * rows, HD)
    scores = mm_t(flat_q, keys).reshape(heads, rows, -1)
    probs = jnp.exp(jnp.where(allowed[None], scores, -1e30) - log_total)
    grad_probs = mm_t(flat_g, values).reshape(heads, rows, -1)
    inner = jnp.sum(probs * grad_probs, axis=-1, keepdims=True)
    grad_scores = (probs * (grad_probs - inner)).astype(BF16).reshape(heads * rows, -1)
    probs_low = probs.astype(BF16).reshape(heads * rows, -1)
    grad_queries = mm(grad_scores, keys).reshape(heads, rows, HD)
    return grad_queries, t_mm(grad_scores, flat_q), t_mm(probs_low, flat_g)


def forward_layer(x, w, place):
    cos, sin, allowed = place
    normed = (x * inverse_rms(x) * w["gain_attn"]).astype(BF16)
    keys = rotate(mm(normed, w["key"]), cos, sin).astype(BF16)
    values = mm(normed, w["value"]).astype(BF16)
    before = from_before(jnp.concatenate([keys, values], axis=1))
    queries = jnp.stack(
        [(rotate(mm(normed, p), cos, sin) * HD**-0.5).astype(BF16) for p in w["query"]]
    )
    keys = jnp.concatenate([before[:, :HD], keys])
    values = jnp.concatenate([before[:, HD:], values])
    mixed, log_total = attend(queries, keys, values, allowed)
    hidden = x
    for j, p in enumerate(w["out"]):
        hidden = hidden + mm(mixed[j], p)
    normed_ff = (hidden * inverse_rms(hidden) * w["gain_ff"]).astype(BF16)
    out = hidden
    gates, ups, acts = [], [], []
    for p_gate, p_up, p_down in zip(w["gate"], w["up"], w["down"]):
        gate, up = mm(normed_ff, p_gate), mm(normed_ff, p_up)
        act = (jax.nn.gelu(gate, approximate=True) * up).astype(BF16)
        out = out + mm(act, p_down)
        gates.append(gate)
        ups.append(up)
        acts.append(act)
    kept = (x, normed, queries, keys, values, mixed, log_total, hidden, normed_ff, gates, ups, acts)
    return out, kept


def ffn_back(grad_out, kept, w):
    hidden, normed_ff, gates, ups, acts = kept[7:]
    g_ff = grad_out.astype(BF16)
    grad_normed = 0.0
    pieces = []
    for j in range(4):
        d_act = mm_t(g_ff, w["down"][j])
        value, slope = gelu_parts(gates[j])
        d_gate = (d_act * ups[j] * slope).astype(BF16)
        d_up = (d_act * value).astype(BF16)
        grad_normed = grad_normed + mm_t(d_gate, w["gate"][j]) + mm_t(d_up, w["up"][j])
        pieces += [t_mm(d_gate, normed_ff), t_mm(d_up, normed_ff), t_mm(acts[j], g_ff)]
    to_hidden, gain_ff = norm_back(hidden, w["gain_ff"], grad_normed)
    return grad_out + to_hidden, gain_ff, [p.astype(BF16) for p in pieces]


def attn_back(grad_hidden, gain_ff, kept, w, place, order):
    cos, sin, allowed = place
    x, normed, queries, keys, values, mixed, log_total = kept[:7]
    g_attn = grad_hidden.astype(BF16)
    grad_mixed = jnp.stack([mm_t(g_attn, p).astype(BF16) for p in w["out"]])
    d_queries, d_keys, d_values = attend_back(
        grad_mixed, queries, keys, values, log_total, allowed
    )
    d_both = jnp.concatenate([d_keys, d_values], axis=1)
    behind = to_before(d_both[:WINDOW].astype(BF16))
    grad_normed = 0.0
    grad_query = []
    for j in range(4):
        d_q = (unrotate(d_queries[j], cos, sin) * HD**-0.5).astype(BF16)
        grad_query.append(t_mm(d_q, normed).astype(BF16))
        grad_normed = grad_normed + mm_t(d_q, w["query"][j])
    grad_out = [t_mm(mixed[j], g_attn).astype(BF16) for j in range(4)]
    d_both = d_both[WINDOW:] + behind.astype(F32)
    d_k = unrotate(d_both[:, :HD], cos, sin).astype(BF16)
    d_v = d_both[:, HD:].astype(BF16)
    grad_normed = grad_normed + mm_t(d_k, w["key"]) + mm_t(d_v, w["value"])
    shared = t_mm(jnp.concatenate([d_k, d_v], axis=1), normed).astype(BF16)
    to_x, gain_attn = norm_back(x, w["gain_attn"], grad_normed)
    gains = jnp.pad(jnp.stack([gain_attn, gain_ff]), ((0, GAIN_ROWS - 2), (0, 0))).astype(BF16)
    count = shared.shape[0] // 4
    pieces = []
    for j in range(4):
        quarter = lax.dynamic_slice_in_dim(shared, (order ^ j) * count, count, 0)
        pieces += [grad_query[j], grad_out[j], quarter, gains]
    return grad_hidden + to_x, pieces


def over_cores(pieces):
    count = len(pieces) // 4
    kept = jnp.concatenate(pieces[: 2 * count])
    kept = kept + swap(jnp.concatenate(pieces[2 * count :]), "gx")
    half = kept.shape[0] // 2
    return kept[:half], kept[half:]


def over_section(total, section):
    half = total.shape[0] // 2
    low, high = total[:half], total[half:]
    return pick(section == 0, low, high) + swap(pick(section == 0, high, low), "section")


def to_owner(value, layer):
    return lax.ppermute(value, "section", [(1 - layer, layer)])


def local(
    x_input,
    doc_lengths,
    cotangent,
    gain_attn,
    w_query,
    w_key,
    w_value,
    w_out,
    gain_ff,
    w_gate,
    w_up,
    w_down,
):
    section = lax.axis_index("section")
    gx, gy = lax.axis_index("gx"), lax.axis_index("gy")
    own_rows = x_input.shape[2]
    scale = 1.0 / lax.axis_size("dp")

    weights = gather_weights(
        w_query[0], w_key[0], w_value[0], w_out[0], w_gate[0], w_up[0], w_down[0], section
    )
    gains = jnp.concatenate([gain_attn, gain_ff])
    other_gains = swap(gains, "section")
    for layer in range(2):
        here = pick(section == layer, gains, other_gains)
        weights[layer]["gain_attn"], weights[layer]["gain_ff"] = here[:1], here[1:]

    lengths = lax.dynamic_index_in_dim(doc_lengths[:, 0], section, 0, keepdims=False)
    x = lax.dynamic_index_in_dim(x_input[:, 0], section, 0, keepdims=False).astype(F32)
    cot = lax.dynamic_index_in_dim(cotangent[:, 0], section, 0, keepdims=False).astype(F32)
    start = (gx * lax.axis_size("gy") + gy) * own_rows
    rows = start - WINDOW + jnp.arange(WINDOW + own_rows, dtype=jnp.int32)
    segment, place, valid = layout(lengths, rows)
    frequency = jnp.exp(jnp.arange(HD // 2, dtype=F32) * (-2.0 * math.log(10000.0) / HD))
    angles = place[WINDOW:].astype(F32)[:, None] * frequency[None, :]
    distance = rows[WINDOW:, None] - rows[None, :]
    allowed = (
        (distance >= 0) & (distance < WINDOW) & (segment[WINDOW:, None] == segment[None, :])
    )
    where = (jnp.cos(angles), jnp.sin(angles), allowed)

    out_0, kept_0 = forward_layer(x, weights[0], where)
    out_0 = out_0.astype(BF16)
    out_1, kept_1 = forward_layer(out_0.astype(F32), weights[1], where)
    out_1 = out_1.astype(BF16)
    states = jnp.where(section == 0, out_0, out_1)
    other_states = swap(jnp.where(section == 0, out_1, out_0), "section")

    order = 2 * gx + gy
    grad_out = cot * valid[WINDOW:, None].astype(F32)
    grad_hidden, gain_ff, pieces = ffn_back(grad_out, kept_1, weights[1])
    ffn_1, far = over_cores(pieces)
    ffn_1 = ffn_1 + swap(far, "gy")
    grad_1, pieces = attn_back(grad_hidden, gain_ff, kept_1, weights[1], where, order)
    grad_1 = grad_1.astype(BF16)
    attn_1, far = over_cores(pieces)
    attn_1 = attn_1 + swap(far, "gy")

    grad_hidden, gain_ff, pieces = ffn_back(grad_1.astype(F32), kept_0, weights[0])
    ffn_1 = over_section(ffn_1, section)
    ffn_0, far = over_cores(pieces)
    grad_hidden, ffn_1, attn_1, ffn_0, far = lax.optimization_barrier(
        (grad_hidden, ffn_1, attn_1, ffn_0, far)
    )
    ffn_0 = ffn_0 + swap(far, "gy")
    ffn_1 = lax.psum(ffn_1, "dp")
    attn_1 = over_section(attn_1, section)
    grad_0, pieces = attn_back(grad_hidden, gain_ff, kept_0, weights[0], where, order)
    grad_0 = grad_0.astype(BF16)
    attn_0, far = over_cores(pieces)
    ffn_1, attn_1, attn_0, far = lax.optimization_barrier((ffn_1, attn_1, attn_0, far))
    attn_1 = lax.psum(attn_1, "dp")
    attn_0 = attn_0 + swap(far, "gy")
    ffn_1_got = to_owner(ffn_1, 1)
    ffn_0 = over_section(ffn_0, section)
    ffn_0, attn_1 = lax.optimization_barrier((ffn_0, attn_1))
    ffn_0 = lax.psum(ffn_0, "dp")
    attn_1_got = to_owner(attn_1, 1)
    attn_0 = over_section(attn_0, section)
    ffn_0, attn_0 = lax.optimization_barrier((ffn_0, attn_0))
    attn_0 = lax.psum(attn_0, "dp")
    ffn_0_got = to_owner(ffn_0, 0)
    attn_0_got = to_owner(attn_0, 0)

    in_grads = pick(section == 0, grad_0, grad_1)
    other_grads = swap(pick(section == 0, grad_1, grad_0), "section")

    def by_micro(own, other):
        first = section == 0
        return jnp.stack([jnp.where(first, own, other), jnp.where(first, other, own)])[
            None, :, None
        ]

    def finished(own_0, got_0, own_1, got_1):
        own, got = pick(section == 0, own_0, own_1), pick(section == 0, got_0, got_1)
        return jnp.concatenate([pick(section == 0, own, got), pick(section == 0, got, own)])

    ffn = finished(ffn_0, ffn_0_got, ffn_1, ffn_1_got)
    attn = finished(attn_0, attn_0_got, attn_1, attn_1_got)
    heads, hidden = w_query.shape[2] // 2, w_gate.shape[2] // 2
    quarter = attn[2 * heads : -GAIN_ROWS]
    quarter_beside = swap(quarter, "gy")
    shared_half = pick(
        gy == 0,
        jnp.concatenate([quarter, quarter_beside]),
        jnp.concatenate([quarter_beside, quarter]),
    )
    gain_sums = attn[-GAIN_ROWS : 2 - GAIN_ROWS].astype(F32) * scale
    ffn_other = swap(ffn, "gx")
    attn_other = swap(jnp.concatenate([attn[: 2 * heads], shared_half]), "gx")

    def both_cores(mine, other):
        low, high = pick(gx == 0, mine, other), pick(gx == 0, other, mine)
        return jnp.concatenate([low, high]).astype(F32) * scale

    gate = both_cores(ffn[:hidden], ffn_other[:hidden]).T
    up = both_cores(ffn[hidden : 2 * hidden], ffn_other[hidden : 2 * hidden]).T
    down = both_cores(ffn[2 * hidden :], ffn_other[2 * hidden :])
    query = both_cores(attn[:heads], attn_other[:heads]).T
    out = both_cores(attn[heads : 2 * heads], attn_other[heads : 2 * heads])
    shared = both_cores(shared_half, attn_other[2 * heads :]).T

    return (
        by_micro(states, other_states),
        by_micro(in_grads, other_grads),
        gain_sums[:1],
        query[None],
        shared[None, :, :HD],
        shared[None, :, HD:],
        out[None],
        gain_sums[1:],
        gate[None],
        up[None],
        down[None],
    )


def solution(mesh):
    rows = P(None, "dp", ("gx", "gy"), None)
    columns = P("section", None, "gy")
    depth = P("section", "gy", None)
    whole = P("section", None, None)
    gain = P("section", None)
    by_layer = P("section", None, "dp", ("gx", "gy"), None)
    return jax.shard_map(
        local,
        mesh=mesh,
        in_specs=(
            rows,
            P(None, "dp", None),
            rows,
            gain,
            columns,
            whole,
            whole,
            depth,
            gain,
            columns,
            columns,
            depth,
        ),
        out_specs=(
            by_layer,
            by_layer,
            gain,
            columns,
            whole,
            whole,
            depth,
            gain,
            columns,
            columns,
            depth,
        ),
        check_vma=False,
    )
```

```python
import math

import jax
import jax.numpy as jnp
from jax import lax
from jax.experimental import pallas as pl
from jax.experimental.pallas import tpu as pltpu
from jax.sharding import PartitionSpec as P

HD = 256
WINDOW = 512
GAIN_ROWS = 32
F32 = jnp.float32
BF16 = jnp.bfloat16


def swap(value, axis):
    return lax.ppermute(value, axis, [(0, 1), (1, 0)])


def mm(a, b):
    return jnp.dot(a, b, preferred_element_type=F32)


def mm_t(a, b):
    return lax.dot_general(a, b, (((1,), (1,)), ((), ())), preferred_element_type=F32)


def t_mm(a, b):
    return lax.dot_general(a, b, (((0,), (0,)), ((), ())), preferred_element_type=F32)


def inverse_rms(value):
    return lax.rsqrt(jnp.mean(value * value, axis=-1, keepdims=True) + 1e-06)


def norm_back(value, gain, grad):
    s = inverse_rms(value)
    scaled = grad * gain
    to_value = s * scaled - value * (s * s * s) * jnp.mean(value * scaled, axis=-1, keepdims=True)
    return to_value, jnp.sum(grad * value * s, axis=0)


def rotate(value, cos, sin):
    half = value.shape[-1] // 2
    a, b = value[..., :half], value[..., half:]
    return jnp.concatenate([a * cos - b * sin, b * cos + a * sin], axis=-1)


def unrotate(value, cos, sin):
    half = value.shape[-1] // 2
    c, e = value[..., :half], value[..., half:]
    return jnp.concatenate([c * cos + e * sin, e * cos - c * sin], axis=-1)


def gelu_parts(v):
    c = math.sqrt(2.0 / math.pi)
    t = jnp.tanh(c * (v + 0.044715 * v * v * v))
    value = 0.5 * v * (1.0 + t)
    slope = 0.5 * (1.0 + t) + 0.5 * v * (1.0 - t * t) * (c * (1.0 + 3 * 0.044715 * v * v))
    return value, slope


def layout(lengths, rows):
    docs = lengths.shape[0]
    ends = jnp.cumsum(lengths)
    number = jnp.sum((rows[:, None] >= ends[None, :]).astype(jnp.int32), axis=1)
    valid = number < docs
    begin = jnp.sum(
        jnp.where(number[:, None] == jnp.arange(docs)[None, :], (ends - lengths)[None, :], 0), axis=1
    )
    place = jnp.where(valid, rows - begin, 0)
    segment = jnp.where(rows < 0, -1, jnp.where(valid, number, docs + rows))
    return segment, place, valid


def pick(flag, a, b):
    return jnp.where(flag, a, b)


def gather_weights(w_query, w_key, w_value, w_out, w_gate, w_up, w_down, section):
    gx = lax.axis_index("gx")

    def half(w, axis):
        size = w.shape[axis] // 2
        return lax.dynamic_slice_in_dim(w, gx * size, size, axis)

    def two_layers(mine, received):
        return [pick(section == layer, mine, received) for layer in range(2)]

    heads = w_query.shape[1] // 2
    first_own = jnp.concatenate([half(w_query, 1), half(w_key, 1), half(w_value, 1)], axis=1)
    out_own = half(w_out, 0)
    wide_own = jnp.concatenate([half(w_gate, 1), half(w_up, 1)], axis=1)
    down_own = half(w_down, 0)
    first_got = swap(first_own, "section")
    down_beside = swap(down_own, "gy")
    out_got = swap(out_own, "section")
    wide_got = swap(wide_own, "section")
    down_own = jnp.concatenate([down_own, down_beside])
    down_got = swap(down_own, "section")

    shared_got = first_got[:, heads:]
    shared_other = swap(shared_got, "gx")
    low, high = pick(gx == 0, shared_got, shared_other), pick(gx == 0, shared_other, shared_got)
    part = low.shape[1] // 2
    key_got = jnp.concatenate([low[:, :part], high[:, :part]], axis=1)
    value_got = jnp.concatenate([low[:, part:], high[:, part:]], axis=1)
    keys, values = two_layers(w_key, key_got), two_layers(w_value, value_got)

    queries = two_layers(first_own[:, :heads], first_got[:, :heads])
    outs = two_layers(out_own, out_got)
    wides = two_layers(wide_own, wide_got)
    downs = two_layers(down_own, down_got)
    layers = []
    for layer in range(2):
        def pairs(own):
            both = jnp.stack([own, swap(own, "gy")])
            return both, swap(both, "gx")

        down = downs[layer].reshape(2, -1, w_down.shape[1])
        layers.append(
            {
                "query": pairs(queries[layer]),
                "out": pairs(outs[layer]),
                "wide": pairs(wides[layer]),
                "down": (down, swap(down, "gx")),
                "key": keys[layer],
                "value": values[layer],
            }
        )
    return layers


def from_before(value):
    return lax.ppermute(value, ("gx", "gy"), [(0, 1), (1, 2), (2, 3)])


def to_before(value):
    return lax.ppermute(value, ("gx", "gy"), [(1, 0), (2, 1), (3, 2)])


BLOCK = 256
STEPS = 4
PARAMS = dict(
    grid=(STEPS,),
    compiler_params=pltpu.CompilerParams(
        dimension_semantics=("arbitrary",), vmem_limit_bytes=56 * 1024 * 1024
    ),
)


def all_of(shape):
    return pl.BlockSpec(shape, lambda j: (0,) * len(shape))


def step_of(shape):
    return pl.BlockSpec((1,) + shape[1:], lambda j: (j,) + (0,) * (len(shape) - 1))


def first_of(shape):
    return pl.BlockSpec((1,) + shape[1:], lambda j: (jnp.minimum(j, 1),) + (0,) * (len(shape) - 1))


def last_of(shape):
    return pl.BlockSpec(
        (1,) + shape[1:], lambda j: (jnp.maximum(j - 2, 0),) + (0,) * (len(shape) - 1)
    )


def cost(flops, bytes_accessed, transcendentals=0):
    return pl.CostEstimate(
        flops=flops, bytes_accessed=bytes_accessed, transcendentals=transcendentals
    )


def take(step, first, last, held):
    @pl.when(step < 2)
    def _():
        held[...] = first[0]

    @pl.when(step >= 2)
    def _():
        held[...] = last[0]


def put_bias(seg_q, seg_k, bias):
    rows, keys = bias.shape
    distance = (
        lax.broadcasted_iota(jnp.int32, (rows, keys), 0)
        + (keys - rows)
        - lax.broadcasted_iota(jnp.int32, (rows, keys), 1)
    )
    allowed = (distance >= 0) & (distance < WINDOW) & (seg_q[...] == seg_k[...])
    bias[...] = jnp.where(allowed, 0.0, -1e30)


def softmax(scores):
    weights = jnp.exp(scores - jnp.max(scores, axis=-1, keepdims=True))
    return weights * (1.0 / jnp.sum(weights, axis=-1, keepdims=True))


def attn_kernel(
    x_ref, gain, wq_a, wq_b, wk, wv, wo_a, wo_b, cos, sin, seg_q, seg_k,
    q_out, mixed_out, kv_out, normed_out, hidden_out, bias, wq, wo,
):
    j = pl.program_id(0)
    rows = normed_out.shape[0]
    before = x_ref.shape[0] - rows

    @pl.when(j == 0)
    def _():
        x = x_ref[...].astype(F32)
        normed = (x * inverse_rms(x) * gain[...]).astype(BF16)
        normed_out[...] = normed[before:]
        kv_out[:, :HD] = rotate(mm(normed, wk[...]), cos[...], sin[...]).astype(BF16)
        kv_out[:, HD:] = mm(normed, wv[...]).astype(BF16)
        hidden_out[...] = x[before:]
        put_bias(seg_q, seg_k, bias)

    take(j, wq_a, wq_b, wq)
    take(j, wo_a, wo_b, wo)
    q = rotate(mm(normed_out[...], wq[...]), cos[before:, :], sin[before:, :]) * HD**-0.5
    q_out[0] = q.astype(BF16)
    for at in range(0, rows, BLOCK):
        here = pl.ds(at, BLOCK)
        keys = pl.ds(at, before + BLOCK)
        scores = mm_t(q_out[0, here, :], kv_out[keys, :HD]) + bias[here, keys]
        mixed = mm(softmax(scores).astype(BF16), kv_out[keys, HD:]).astype(BF16)
        mixed_out[0, here, :] = mixed
        hidden_out[here, :] += mm(mixed, wo[...])


def attn_forward(x_all, w, place):
    cos, sin, seg_q, seg_k = place
    total, width = x_all.shape
    rows = seg_q.shape[0]
    heads = (STEPS, rows, HD)
    ops = (x_all, w["gain_attn"], *w["query"], w["key"], w["value"], *w["out"], cos, sin, seg_q, seg_k)
    pairs = {2: first_of, 3: last_of, 6: first_of, 7: last_of}
    return pl.pallas_call(
        attn_kernel,
        out_shape=(
            jax.ShapeDtypeStruct(heads, BF16),
            jax.ShapeDtypeStruct(heads, BF16),
            jax.ShapeDtypeStruct((total, 2 * HD), BF16),
            jax.ShapeDtypeStruct((rows, width), BF16),
            jax.ShapeDtypeStruct((rows, width), F32),
        ),
        in_specs=[pairs.get(i, all_of)(op.shape) for i, op in enumerate(ops)],
        out_specs=(
            step_of(heads),
            step_of(heads),
            all_of((total, 2 * HD)),
            all_of((rows, width)),
            all_of((rows, width)),
        ),
        scratch_shapes=[
            pltpu.VMEM((rows, total), F32),
            pltpu.VMEM((width, HD), BF16),
            pltpu.VMEM((HD, width), BF16),
        ],
        cost_estimate=cost(8 * 10**9, 12 * 10**6, 2 * 10**6),
        **PARAMS,
    )(*ops)


def ffn_kernel(hidden, gain, wide_a, wide_b, down_a, down_b, out, normed, total, wide, down):
    j = pl.program_id(0)
    units = down.shape[0]

    @pl.when(j == 0)
    def _():
        value = hidden[...]
        normed[...] = (value * inverse_rms(value) * gain[...]).astype(BF16)
        total[...] = value

    take(j, wide_a, wide_b, wide)
    take(j, down_a, down_b, down)
    gate = mm(normed[...], wide[:, :units])
    up = mm(normed[...], wide[:, units:])
    act = (gelu_parts(gate)[0] * up).astype(BF16)
    total[...] += mm(act, down[...])

    @pl.when(j == STEPS - 1)
    def _():
        out[...] = total[...].astype(BF16)


def ffn_forward(hidden, w):
    rows, width = hidden.shape
    ops = (hidden, w["gain_ff"], *w["wide"], *w["down"])
    units = w["down"][0].shape[1]
    pairs = {2: first_of, 3: last_of, 4: first_of, 5: last_of}
    return pl.pallas_call(
        ffn_kernel,
        out_shape=jax.ShapeDtypeStruct((rows, width), BF16),
        in_specs=[pairs.get(i, all_of)(op.shape) for i, op in enumerate(ops)],
        out_specs=all_of((rows, width)),
        scratch_shapes=[
            pltpu.VMEM((rows, width), BF16),
            pltpu.VMEM((rows, width), F32),
            pltpu.VMEM((width, 2 * units), BF16),
            pltpu.VMEM((units, width), BF16),
        ],
        cost_estimate=cost(8 * 10**9, 12 * 10**6, 10**6),
        **PARAMS,
    )(*ops)


def ffn_back_kernel(
    dy, hidden, gain, wide_a, wide_b, down_a, down_b,
    near, far, d_hidden, d_gain, normed, total, wide, down,
):
    j = pl.program_id(0)
    units = down.shape[0]

    @pl.when(j == 0)
    def _():
        value = hidden[...]
        normed[...] = (value * inverse_rms(value) * gain[...]).astype(BF16)
        total[...] = jnp.zeros_like(total)

    take(j, wide_a, wide_b, wide)
    take(j, down_a, down_b, down)
    gate = mm(normed[...], wide[:, :units])
    up = mm(normed[...], wide[:, units:])
    d_act = mm_t(dy[...], down[...])
    value, slope = gelu_parts(gate)
    act = (value * up).astype(BF16)
    d_gate = (d_act * up * slope).astype(BF16)
    d_up = (d_act * value).astype(BF16)
    total[...] += mm_t(d_gate, wide[:, :units]) + mm_t(d_up, wide[:, units:])
    parts = [t_mm(d_gate, normed[...]), t_mm(d_up, normed[...]), t_mm(act, dy[...])]

    def put(out):
        for i, part in enumerate(parts):
            out[0, pl.ds(i * units, units), :] = part.astype(BF16)

    pl.when(j < 2)(lambda: put(near))
    pl.when(j >= 2)(lambda: put(far))

    @pl.when(j == STEPS - 1)
    def _():
        to_hidden, to_gain = norm_back(hidden[...], gain[...], total[...])
        d_hidden[...] = dy[...].astype(F32) + to_hidden
        d_gain[...] = to_gain[None]


def ffn_back(dy, hidden, w):
    rows, width = hidden.shape
    ops = (dy, hidden, w["gain_ff"], *w["wide"], *w["down"])
    units = w["down"][0].shape[1]
    pairs = {3: first_of, 4: last_of, 5: first_of, 6: last_of}
    packed = (2, 3 * units, width)
    return pl.pallas_call(
        ffn_back_kernel,
        out_shape=(
            jax.ShapeDtypeStruct(packed, BF16),
            jax.ShapeDtypeStruct(packed, BF16),
            jax.ShapeDtypeStruct((rows, width), F32),
            jax.ShapeDtypeStruct((1, width), F32),
        ),
        in_specs=[pairs.get(i, all_of)(op.shape) for i, op in enumerate(ops)],
        out_specs=(first_of(packed), last_of(packed), all_of((rows, width)), all_of((1, width))),
        scratch_shapes=[
            pltpu.VMEM((rows, width), BF16),
            pltpu.VMEM((rows, width), F32),
            pltpu.VMEM((width, 2 * units), BF16),
            pltpu.VMEM((units, width), BF16),
        ],
        cost_estimate=cost(16 * 10**9, 24 * 10**6, 10**6),
        **PARAMS,
    )(*ops)


def attn_back_kernel(
    d_hidden, q, mixed, kv, wo_a, wo_b, cos, sin, seg_q, seg_k,
    d_out, d_q, d_kv, bias, wo, grad,
):
    j = pl.program_id(0)
    rows = grad.shape[0]
    before = kv.shape[0] - rows

    @pl.when(j == 0)
    def _():
        grad[...] = d_hidden[...].astype(BF16)
        d_kv[...] = jnp.zeros_like(d_kv)
        put_bias(seg_q, seg_k, bias)

    take(j, wo_a, wo_b, wo)
    d_out[0] = t_mm(mixed[0], grad[...]).astype(BF16)
    for at in range(0, rows, BLOCK):
        here = pl.ds(at, BLOCK)
        keys = pl.ds(at, before + BLOCK)
        q_here = q[0, here, :]
        d_mixed = mm_t(grad[here, :], wo[...]).astype(BF16)
        probs = softmax(mm_t(q_here, kv[keys, :HD]) + bias[here, keys])
        d_probs = mm_t(d_mixed, kv[keys, HD:])
        inner = jnp.sum(probs * d_probs, axis=-1, keepdims=True)
        d_scores = (probs * (d_probs - inner)).astype(BF16)
        back = unrotate(mm(d_scores, kv[keys, :HD]), cos[here, :], sin[here, :]) * HD**-0.5
        d_q[0, here, :] = back.astype(BF16)
        d_kv[keys, :HD] += t_mm(d_scores, q_here)
        d_kv[keys, HD:] += t_mm(probs.astype(BF16), d_mixed)


def attn_back(d_hidden, q, mixed, kv, w, place):
    cos, sin, seg_q, seg_k = place
    rows, width = d_hidden.shape
    total = kv.shape[0]
    cos, sin = cos[total - rows :], sin[total - rows :]
    ops = (d_hidden, q, mixed, kv, *w["out"], cos, sin, seg_q, seg_k)
    pairs = {1: step_of, 2: step_of, 4: first_of, 5: last_of}
    outs = (STEPS, HD, width)
    return pl.pallas_call(
        attn_back_kernel,
        out_shape=(
            jax.ShapeDtypeStruct(outs, BF16),
            jax.ShapeDtypeStruct(q.shape, BF16),
            jax.ShapeDtypeStruct((total, 2 * HD), F32),
        ),
        in_specs=[pairs.get(i, all_of)(op.shape) for i, op in enumerate(ops)],
        out_specs=(step_of(outs), step_of(q.shape), all_of((total, 2 * HD))),
        scratch_shapes=[
            pltpu.VMEM((rows, total), F32),
            pltpu.VMEM((HD, width), BF16),
            pltpu.VMEM((rows, width), BF16),
        ],
        cost_estimate=cost(10 * 10**9, 12 * 10**6, 2 * 10**6),
        **PARAMS,
    )(*ops)


def query_back_kernel(d_q, normed, wq_a, wq_b, d_query, d_normed, wq):
    j = pl.program_id(0)
    take(j, wq_a, wq_b, wq)
    d_query[0] = t_mm(d_q[0], normed[...]).astype(BF16)
    term = mm_t(d_q[0], wq[...])

    @pl.when(j == 0)
    def _():
        d_normed[...] = term

    @pl.when(j > 0)
    def _():
        d_normed[...] += term


def query_back(d_q, normed, w):
    rows, width = normed.shape
    ops = (d_q, normed, *w["query"])
    outs = (STEPS, HD, width)
    pairs = {0: step_of, 2: first_of, 3: last_of}
    return pl.pallas_call(
        query_back_kernel,
        out_shape=(jax.ShapeDtypeStruct(outs, BF16), jax.ShapeDtypeStruct((rows, width), F32)),
        in_specs=[pairs.get(i, all_of)(op.shape) for i, op in enumerate(ops)],
        out_specs=(step_of(outs), all_of((rows, width))),
        scratch_shapes=[pltpu.VMEM((width, HD), BF16)],
        cost_estimate=cost(2 * 10**9, 6 * 10**6),
        **PARAMS,
    )(*ops)


def input_back_kernel(
    d_kv, behind, normed, wk, wv, d_normed, x_ref, gain, d_hidden, cos, sin, d_x, d_shared, d_gain
):
    total = d_kv[...] + behind[...].astype(F32)
    d_k = unrotate(total[:, :HD], cos[...], sin[...]).astype(BF16)
    d_v = total[:, HD:].astype(BF16)
    d_shared[:HD, :] = t_mm(d_k, normed[...]).astype(BF16)
    d_shared[HD:, :] = t_mm(d_v, normed[...]).astype(BF16)
    grad = d_normed[...] + mm_t(d_k, wk[...]) + mm_t(d_v, wv[...])
    to_x, to_gain = norm_back(x_ref[...].astype(F32), gain[...], grad)
    d_x[...] = (d_hidden[...] + to_x).astype(BF16)
    d_gain[...] = to_gain[None]


def input_back(d_kv, behind, normed, d_normed, x, d_hidden, w, place):
    cos, sin = place[:2]
    rows, width = normed.shape
    before = cos.shape[0] - rows
    ops = (
        d_kv[before:], behind, normed, w["key"], w["value"], d_normed, x, w["gain_attn"], d_hidden,
        cos[before:], sin[before:],
    )
    return pl.pallas_call(
        input_back_kernel,
        out_shape=(
            jax.ShapeDtypeStruct((rows, width), BF16),
            jax.ShapeDtypeStruct((2 * HD, width), BF16),
            jax.ShapeDtypeStruct((1, width), F32),
        ),
        compiler_params=pltpu.CompilerParams(vmem_limit_bytes=56 * 1024 * 1024),
        cost_estimate=cost(10**9, 8 * 10**6),
    )(*ops)


def pack_attn(d_query, d_out, d_shared, d_gain_attn, d_gain_ff, order):
    gains = jnp.concatenate([d_gain_attn, d_gain_ff])
    gains = jnp.pad(gains, ((0, GAIN_ROWS - 2), (0, 0))).astype(BF16)
    count = d_shared.shape[0] // STEPS
    pieces = []
    for j in range(STEPS):
        quarter = lax.dynamic_slice_in_dim(d_shared, (order ^ j) * count, count, 0)
        pieces.append(jnp.concatenate([d_query[j], d_out[j], quarter, gains]))
    return jnp.stack(pieces[:2]), jnp.stack(pieces[2:])


def over_cores(near, far):
    kept = near + swap(far, "gx")
    return kept[0], kept[1]


def over_section(total, section):
    half = total.shape[0] // 2
    low, high = total[:half], total[half:]
    return pick(section == 0, low, high) + swap(pick(section == 0, high, low), "section")


def to_owner(value, layer):
    return lax.ppermute(value, "section", [(1 - layer, layer)])


def local(
    x_input,
    doc_lengths,
    cotangent,
    gain_attn,
    w_query,
    w_key,
    w_value,
    w_out,
    gain_ff,
    w_gate,
    w_up,
    w_down,
):
    section = lax.axis_index("section")
    gx, gy = lax.axis_index("gx"), lax.axis_index("gy")
    own_rows = x_input.shape[2]
    scale = 1.0 / lax.axis_size("dp")

    weights = gather_weights(
        w_query[0], w_key[0], w_value[0], w_out[0], w_gate[0], w_up[0], w_down[0], section
    )
    gains = jnp.concatenate([gain_attn, gain_ff])
    other_gains = swap(gains, "section")
    for layer in range(2):
        here = pick(section == layer, gains, other_gains)
        weights[layer]["gain_attn"], weights[layer]["gain_ff"] = here[:1], here[1:]

    def mine(value):
        return lax.dynamic_index_in_dim(value[:, 0], section, 0, keepdims=False)

    x = mine(x_input)
    x_all = jnp.concatenate([from_before(x), x])
    start = (gx * lax.axis_size("gy") + gy) * own_rows
    rows = start - WINDOW + jnp.arange(WINDOW + own_rows, dtype=jnp.int32)
    segment, where_in, valid = layout(mine(doc_lengths), rows)
    frequency = jnp.exp(jnp.arange(HD // 2, dtype=F32) * (-2.0 * math.log(10000.0) / HD))
    angles = where_in.astype(F32)[:, None] * frequency[None, :]
    place = (jnp.cos(angles), jnp.sin(angles), segment[WINDOW:, None], segment[None, :])

    q_0, mixed_0, kv_0, normed_0, hidden_0 = attn_forward(x_all, weights[0], place)
    out_0 = ffn_forward(hidden_0, weights[0])
    out_all = jnp.concatenate([from_before(out_0), out_0])
    q_1, mixed_1, kv_1, normed_1, hidden_1 = attn_forward(out_all, weights[1], place)
    out_1 = ffn_forward(hidden_1, weights[1])
    states = pick(section == 0, out_0, out_1)
    other_states = swap(pick(section == 0, out_1, out_0), "section")

    order = 2 * gx + gy
    barrier = lax.optimization_barrier
    dy = jnp.where(valid[WINDOW:, None], mine(cotangent), 0)

    near, far, d_hidden, gain_ff = ffn_back(dy, hidden_1, weights[1])
    ffn_1, ffn_far_1 = over_cores(near, far)
    d_out, d_q, d_kv = attn_back(d_hidden, q_1, mixed_1, kv_1, weights[1], place)
    d_q, d_kv, ffn_1, ffn_far_1 = barrier((d_q, d_kv, ffn_1, ffn_far_1))
    ffn_got = swap(ffn_far_1, "gy")
    behind = to_before(d_kv[:WINDOW].astype(BF16))
    d_query, d_normed = query_back(d_q, normed_1, weights[1])
    grad_1, d_shared, gain_attn_grad = input_back(
        d_kv, behind, normed_1, d_normed, out_0, d_hidden, weights[1], place
    )
    attn_1, attn_far_1 = over_cores(
        *pack_attn(d_query, d_out, d_shared, gain_attn_grad, gain_ff, order)
    )

    near, far, d_hidden, gain_ff = ffn_back(grad_1, hidden_0, weights[0])
    d_hidden, near, far, ffn_got, attn_1, attn_far_1 = barrier(
        (d_hidden, near, far, ffn_got, attn_1, attn_far_1)
    )
    ffn_1 = over_section(ffn_1 + ffn_got, section)
    attn_1 = attn_1 + swap(attn_far_1, "gy")
    ffn_0, ffn_far_0 = over_cores(near, far)
    d_out, d_q, d_kv = attn_back(d_hidden, q_0, mixed_0, kv_0, weights[0], place)
    d_q, d_kv, attn_1, ffn_0, ffn_far_0 = barrier((d_q, d_kv, attn_1, ffn_0, ffn_far_0))
    ffn_0 = ffn_0 + swap(ffn_far_0, "gy")
    behind = to_before(d_kv[:WINDOW].astype(BF16))
    d_query, d_normed = query_back(d_q, normed_0, weights[0])
    grad_0, d_shared, gain_attn_grad = input_back(
        d_kv, behind, normed_0, d_normed, x, d_hidden, weights[0], place
    )
    attn_1 = over_section(attn_1, section)
    grad_0, ffn_1, attn_1 = barrier((grad_0, ffn_1, attn_1))
    layer_1 = lax.psum(jnp.concatenate([ffn_1, attn_1]), "dp")
    attn_0, far = over_cores(*pack_attn(d_query, d_out, d_shared, gain_attn_grad, gain_ff, order))
    attn_0 = attn_0 + swap(far, "gy")
    ffn_0 = over_section(ffn_0, section)
    attn_0 = over_section(attn_0, section)
    layer_1, ffn_0, attn_0 = barrier((layer_1, ffn_0, attn_0))
    layer_1_got = to_owner(layer_1, 1)
    layer_0 = lax.psum(jnp.concatenate([ffn_0, attn_0]), "dp")
    layer_0_got = to_owner(layer_0, 0)
    split = ffn_0.shape[0]

    in_grads = pick(section == 0, grad_0, grad_1)
    other_grads = swap(pick(section == 0, grad_1, grad_0), "section")

    def by_micro(own, other):
        first = section == 0
        return jnp.stack([jnp.where(first, own, other), jnp.where(first, other, own)])[
            None, :, None
        ]

    def finished(own_0, got_0, own_1, got_1):
        own, got = pick(section == 0, own_0, own_1), pick(section == 0, got_0, got_1)
        return jnp.concatenate([pick(section == 0, own, got), pick(section == 0, got, own)])

    def part(lo, hi):
        return finished(
            layer_0[lo:hi], layer_0_got[lo:hi], layer_1[lo:hi], layer_1_got[lo:hi]
        )

    ffn, attn = part(0, split), part(split, None)
    heads, hidden = w_query.shape[2] // 2, w_gate.shape[2] // 2
    quarter = attn[2 * heads : -GAIN_ROWS]
    quarter_beside = swap(quarter, "gy")
    shared_half = pick(
        gy == 0,
        jnp.concatenate([quarter, quarter_beside]),
        jnp.concatenate([quarter_beside, quarter]),
    )
    gain_sums = attn[-GAIN_ROWS : 2 - GAIN_ROWS].astype(F32) * scale
    ffn_other = swap(ffn, "gx")
    attn_other = swap(jnp.concatenate([attn[: 2 * heads], shared_half]), "gx")

    def both_cores(mine, other):
        low, high = pick(gx == 0, mine, other), pick(gx == 0, other, mine)
        return jnp.concatenate([low, high]).astype(F32) * scale

    gate = both_cores(ffn[:hidden], ffn_other[:hidden]).T
    up = both_cores(ffn[hidden : 2 * hidden], ffn_other[hidden : 2 * hidden]).T
    down = both_cores(ffn[2 * hidden :], ffn_other[2 * hidden :])
    query = both_cores(attn[:heads], attn_other[:heads]).T
    out = both_cores(attn[heads : 2 * heads], attn_other[heads : 2 * heads])
    shared = both_cores(shared_half, attn_other[2 * heads :]).T

    return (
        by_micro(states, other_states),
        by_micro(in_grads, other_grads),
        gain_sums[:1],
        query[None],
        shared[None, :, :HD],
        shared[None, :, HD:],
        out[None],
        gain_sums[1:],
        gate[None],
        up[None],
        down[None],
    )


def solution(mesh):
    rows = P(None, "dp", ("gx", "gy"), None)
    columns = P("section", None, "gy")
    depth = P("section", "gy", None)
    whole = P("section", None, None)
    gain = P("section", None)
    by_layer = P("section", None, "dp", ("gx", "gy"), None)
    return jax.shard_map(
        local,
        mesh=mesh,
        in_specs=(
            rows,
            P(None, "dp", None),
            rows,
            gain,
            columns,
            whole,
            whole,
            depth,
            gain,
            columns,
            columns,
            depth,
        ),
        out_specs=(
            by_layer,
            by_layer,
            gain,
            columns,
            whole,
            whole,
            depth,
            gain,
            columns,
            columns,
            depth,
        ),
        check_vma=False,
    )
```

```python
import functools
import math

import jax
import jax.numpy as jnp
from jax import lax
from jax.experimental import pallas as pl
from jax.experimental.pallas import tpu as pltpu
from jax.sharding import PartitionSpec as P

HD = 256
WINDOW = 512
GAIN_ROWS = 32
F32 = jnp.float32
BF16 = jnp.bfloat16


def swap(value, axis):
    return lax.ppermute(value, axis, [(0, 1), (1, 0)])


def mm(a, b):
    return jnp.dot(a, b, preferred_element_type=F32)


def mm_t(a, b):
    return lax.dot_general(a, b, (((1,), (1,)), ((), ())), preferred_element_type=F32)


def t_mm(a, b):
    return lax.dot_general(a, b, (((0,), (0,)), ((), ())), preferred_element_type=F32)


def inverse_rms(value):
    return lax.rsqrt(jnp.mean(value * value, axis=-1, keepdims=True) + 1e-06)


def norm_back(value, gain, grad):
    s = inverse_rms(value)
    scaled = grad * gain
    to_value = s * scaled - value * (s * s * s) * jnp.mean(value * scaled, axis=-1, keepdims=True)
    return to_value, jnp.sum(grad * value * s, axis=0)


def rotate(value, cos, sin):
    half = value.shape[-1] // 2
    a, b = value[..., :half], value[..., half:]
    return jnp.concatenate([a * cos - b * sin, b * cos + a * sin], axis=-1)


def unrotate(value, cos, sin):
    half = value.shape[-1] // 2
    c, e = value[..., :half], value[..., half:]
    return jnp.concatenate([c * cos + e * sin, e * cos - c * sin], axis=-1)


def gelu_parts(v):
    c = math.sqrt(2.0 / math.pi)
    t = jnp.tanh(c * (v + 0.044715 * v * v * v))
    value = 0.5 * v * (1.0 + t)
    slope = 0.5 * (1.0 + t) + 0.5 * v * (1.0 - t * t) * (c * (1.0 + 3 * 0.044715 * v * v))
    return value, slope


def layout(lengths, rows):
    docs = lengths.shape[0]
    ends = jnp.cumsum(lengths)
    number = jnp.sum((rows[:, None] >= ends[None, :]).astype(jnp.int32), axis=1)
    valid = number < docs
    begin = jnp.sum(
        jnp.where(number[:, None] == jnp.arange(docs)[None, :], (ends - lengths)[None, :], 0), axis=1
    )
    place = jnp.where(valid, rows - begin, 0)
    segment = jnp.where(rows < 0, -1, jnp.where(valid, number, docs + rows))
    return segment, place, valid


def pick(flag, a, b):
    return jnp.where(flag, a, b)


def gather_weights(x, w_query, w_key, w_value, w_out, w_gate, w_up, w_down, section):
    gx = lax.axis_index("gx")
    barrier = lax.optimization_barrier

    def half(w, axis):
        size = w.shape[axis] // 2
        return lax.dynamic_slice_in_dim(w, gx * size, size, axis)

    def two_layers(mine, received):
        return [pick(section == layer, mine, received) for layer in range(2)]

    def over_gx(own, beside):
        both = jnp.stack([own, beside])
        return both, swap(both, "gx")

    heads = w_query.shape[1] // 2
    first_own = jnp.concatenate([half(w_query, 1), half(w_key, 1), half(w_value, 1)], axis=1)
    out_own, gate_own, up_own, down_own = half(w_out, 0), half(w_gate, 1), half(w_up, 1), half(w_down, 0)
    first_got = swap(first_own, "section")
    x_before = from_before(x)
    out_got = swap(out_own, "section")
    down_beside = swap(down_own, "gy")
    first_got, gate_own = barrier((first_got, gate_own))

    queries = two_layers(first_own[:, :heads], first_got[:, :heads])
    query_beside = swap(queries[0], "gy")
    gate_got = swap(gate_own, "section")
    shared_got = first_got[:, heads:]
    shared_other = swap(shared_got, "gx")
    out_got, up_own = barrier((out_got, up_own))

    outs = two_layers(out_own, out_got)
    out_beside = swap(outs[0], "gy")
    up_got = swap(up_own, "section")
    low, high = pick(gx == 0, shared_got, shared_other), pick(gx == 0, shared_other, shared_got)
    part = low.shape[1] // 2
    key_got = jnp.concatenate([low[:, :part], high[:, :part]], axis=1)
    value_got = jnp.concatenate([low[:, part:], high[:, part:]], axis=1)
    keys, values = two_layers(w_key, key_got), two_layers(w_value, value_got)
    down_pair = jnp.stack([down_own, down_beside])
    gate_got, down_pair, keys, values = barrier((gate_got, down_pair, keys, values))

    gates = two_layers(gate_own, gate_got)
    gate_beside = swap(gates[0], "gy")
    down_got = swap(down_pair, "section")
    query_beside, out_beside, x_before, up_got = barrier((query_beside, out_beside, x_before, up_got))
    ups = two_layers(up_own, up_got)
    up_beside = swap(ups[0], "gy")
    later = queries[1], outs[1]
    later_besides = [swap(value, "gy") for value in later]
    first = {
        "query": over_gx(queries[0], query_beside),
        "out": over_gx(outs[0], out_beside),
        "key": keys[0],
        "value": values[0],
    }

    def finish(kernel_out):
        kernel_out, gate_here, up_here, arrived, gate_1 = barrier(
            (kernel_out, gate_beside, up_beside, later_besides, gates[1])
        )
        gate_1_beside = swap(gate_1, "gy")
        downs = two_layers(down_pair, down_got)
        first.update(
            gate=over_gx(gates[0], gate_here),
            up=over_gx(ups[0], up_here),
            down=(downs[0], swap(downs[0], "gx")),
        )

        def second(kernel_out):
            kernel_out, gate_1_here, up_1, down_1 = barrier(
                (kernel_out, gate_1_beside, ups[1], downs[1])
            )
            rows_before = from_before(kernel_out)
            gate_pairs = over_gx(gate_1, gate_1_here)
            down_pairs = down_1, swap(down_1, "gx")
            query_pairs, out_pairs = over_gx(later[0], arrived[0]), over_gx(later[1], arrived[1])
            rows_before, up_1 = barrier((rows_before, up_1))
            layer = {
                "query": query_pairs,
                "out": out_pairs,
                "gate": gate_pairs,
                "up": (up_1, swap(up_1, "gy")),
                "down": down_pairs,
                "key": keys[1],
                "value": values[1],
            }
            return kernel_out, rows_before, layer

        return kernel_out, second

    return first, x_before, finish


def from_before(value):
    return lax.ppermute(value, ("gx", "gy"), [(0, 1), (1, 2), (2, 3)])


def to_before(value):
    return lax.ppermute(value, ("gx", "gy"), [(1, 0), (2, 1), (3, 2)])


BLOCK = 256
STEPS = 4
PARAMS = dict(
    grid=(STEPS,),
    compiler_params=pltpu.CompilerParams(
        dimension_semantics=("arbitrary",), vmem_limit_bytes=56 * 1024 * 1024
    ),
)


def all_of(shape):
    return pl.BlockSpec(shape, lambda j: (0,) * len(shape))


def step_of(shape):
    return pl.BlockSpec((1,) + shape[1:], lambda j: (j,) + (0,) * (len(shape) - 1))


def first_of(shape):
    return pl.BlockSpec((1,) + shape[1:], lambda j: (jnp.minimum(j, 1),) + (0,) * (len(shape) - 1))


def last_of(shape):
    return pl.BlockSpec(
        (1,) + shape[1:], lambda j: (jnp.maximum(j - 2, 0),) + (0,) * (len(shape) - 1)
    )


SMALL = pl.CostEstimate(flops=1000, bytes_accessed=1000, transcendentals=0)


def take(step, first, last, held):
    @pl.when(step < 2)
    def _():
        held[...] = first[0]

    @pl.when(step >= 2)
    def _():
        held[...] = last[0]


def put_bias(seg_q, seg_k, bias):
    rows, keys = bias.shape
    distance = (
        lax.broadcasted_iota(jnp.int32, (rows, keys), 0)
        + (keys - rows)
        - lax.broadcasted_iota(jnp.int32, (rows, keys), 1)
    )
    allowed = (distance >= 0) & (distance < WINDOW) & (seg_q[...] == seg_k[...])
    bias[...] = jnp.where(allowed, 0.0, -1e30)


def softmax(scores):
    weights = jnp.exp(scores - jnp.max(scores, axis=-1, keepdims=True))
    return weights * (1.0 / jnp.sum(weights, axis=-1, keepdims=True))


def attn_kernel(
    x_ref, gain, wq_a, wq_b, wk, wv, wo_a, wo_b, cos, sin, seg_q, seg_k,
    q_out, mixed_out, kv_out, normed_out, hidden_out, bias, wq, wo,
):
    j = pl.program_id(0)
    rows = normed_out.shape[0]
    before = x_ref.shape[0] - rows

    @pl.when(j == 0)
    def _():
        x = x_ref[...].astype(F32)
        normed = (x * inverse_rms(x) * gain[...]).astype(BF16)
        normed_out[...] = normed[before:]
        kv_out[:, :HD] = rotate(mm(normed, wk[...]), cos[...], sin[...]).astype(BF16)
        kv_out[:, HD:] = mm(normed, wv[...]).astype(BF16)
        hidden_out[...] = x[before:]
        put_bias(seg_q, seg_k, bias)

    take(j, wq_a, wq_b, wq)
    take(j, wo_a, wo_b, wo)
    q = rotate(mm(normed_out[...], wq[...]), cos[before:, :], sin[before:, :]) * HD**-0.5
    q_out[0] = q.astype(BF16)
    for at in range(0, rows, BLOCK):
        here = pl.ds(at, BLOCK)
        keys = pl.ds(at, before + BLOCK)
        scores = mm_t(q_out[0, here, :], kv_out[keys, :HD]) + bias[here, keys]
        mixed = mm(softmax(scores).astype(BF16), kv_out[keys, HD:]).astype(BF16)
        mixed_out[0, here, :] = mixed
        hidden_out[here, :] += mm(mixed, wo[...])


def attn_forward(x_all, w, place):
    cos, sin, seg_q, seg_k = place
    total, width = x_all.shape
    rows = seg_q.shape[0]
    heads = (STEPS, rows, HD)
    ops = (x_all, w["gain_attn"], *w["query"], w["key"], w["value"], *w["out"], cos, sin, seg_q, seg_k)
    pairs = {2: first_of, 3: last_of, 6: first_of, 7: last_of}
    return pl.pallas_call(
        attn_kernel,
        out_shape=(
            jax.ShapeDtypeStruct(heads, BF16),
            jax.ShapeDtypeStruct(heads, BF16),
            jax.ShapeDtypeStruct((total, 2 * HD), BF16),
            jax.ShapeDtypeStruct((rows, width), BF16),
            jax.ShapeDtypeStruct((rows, width), F32),
        ),
        in_specs=[pairs.get(i, all_of)(op.shape) for i, op in enumerate(ops)],
        out_specs=(
            step_of(heads),
            step_of(heads),
            all_of((total, 2 * HD)),
            all_of((rows, width)),
            all_of((rows, width)),
        ),
        scratch_shapes=[
            pltpu.VMEM((rows, total), F32),
            pltpu.VMEM((width, HD), BF16),
            pltpu.VMEM((HD, width), BF16),
        ],
        cost_estimate=SMALL,
        **PARAMS,
    )(*ops)


def ffn_kernel(
    hidden, gain, gate_a, gate_b, up_a, up_b, down_a, down_b,
    out, normed, total, w_gate, w_up, down,
):
    j = pl.program_id(0)

    @pl.when(j == 0)
    def _():
        value = hidden[...]
        normed[...] = (value * inverse_rms(value) * gain[...]).astype(BF16)
        total[...] = value

    take(j, gate_a, gate_b, w_gate)
    take(j, up_a, up_b, w_up)
    take(j, down_a, down_b, down)
    gate = mm(normed[...], w_gate[...])
    up = mm(normed[...], w_up[...])
    act = (gelu_parts(gate)[0] * up).astype(BF16)
    total[...] += mm(act, down[...])

    @pl.when(j == STEPS - 1)
    def _():
        out[...] = total[...].astype(BF16)


def ffn_forward(hidden, w):
    rows, width = hidden.shape
    ops = (hidden, w["gain_ff"], *w["gate"], *w["up"], *w["down"])
    units = w["down"][0].shape[1]
    pairs = {i: (first_of, last_of)[i % 2] for i in range(2, 8)}
    return pl.pallas_call(
        ffn_kernel,
        out_shape=jax.ShapeDtypeStruct((rows, width), BF16),
        in_specs=[pairs.get(i, all_of)(op.shape) for i, op in enumerate(ops)],
        out_specs=all_of((rows, width)),
        scratch_shapes=[
            pltpu.VMEM((rows, width), BF16),
            pltpu.VMEM((rows, width), F32),
            pltpu.VMEM((width, units), BF16),
            pltpu.VMEM((width, units), BF16),
            pltpu.VMEM((units, width), BF16),
        ],
        cost_estimate=SMALL,
        **PARAMS,
    )(*ops)


def ffn_back_kernel(last, dy, hidden, gain, before, gate, up, down, out, *rest):
    total, normed = rest[-2:]
    j = pl.program_id(0)
    units = down.shape[1]

    @pl.when(j == 0)
    def _():
        value = hidden[...]
        normed[...] = (value * inverse_rms(value) * gain[...]).astype(BF16)
        total[...] = before[...] if last else jnp.zeros_like(total)

    gate_value = mm(normed[...], gate[0])
    up_value = mm(normed[...], up[0])
    d_act = mm_t(dy[...], down[0])
    value, slope = gelu_parts(gate_value)
    act = (value * up_value).astype(BF16)
    d_gate = (d_act * up_value * slope).astype(BF16)
    d_up = (d_act * value).astype(BF16)
    total[...] += mm_t(d_gate, gate[0]) + mm_t(d_up, up[0])
    for i, part in enumerate((t_mm(d_gate, normed[...]), t_mm(d_up, normed[...]), t_mm(act, dy[...]))):
        out[0, pl.ds(i * units, units), :] = part.astype(BF16)

    @pl.when(j == pl.num_programs(0) - 1)
    def _():
        if last:
            d_hidden, d_gain = rest[:2]
            to_hidden, to_gain = norm_back(hidden[...], gain[...], total[...])
            d_hidden[...] = dy[...].astype(F32) + to_hidden
            d_gain[...] = to_gain[None]
        else:
            rest[0][...] = total[...]


def ffn_back(dy, hidden, w, pair, before=None):
    rows, width = hidden.shape
    last = before is not None
    ops = (dy, hidden, w["gain_ff"], before if last else jnp.zeros((8, 128), F32))
    ops += (w["gate"][pair], w["up"][pair], w["down"][pair])
    packed = (2, 3 * w["down"][pair].shape[1], width)
    shapes = [(rows, width), (1, width)] if last else [(rows, width)]
    return pl.pallas_call(
        functools.partial(ffn_back_kernel, last),
        grid=(2,),
        out_shape=[jax.ShapeDtypeStruct(packed, BF16)]
        + [jax.ShapeDtypeStruct(shape, F32) for shape in shapes],
        in_specs=[all_of(op.shape) for op in ops[:4]] + [step_of(op.shape) for op in ops[4:]],
        out_specs=[step_of(packed)] + [all_of(shape) for shape in shapes],
        scratch_shapes=[pltpu.VMEM((rows, width), F32), pltpu.VMEM((rows, width), BF16)],
        compiler_params=pltpu.CompilerParams(
            dimension_semantics=("arbitrary",), vmem_limit_bytes=56 * 1024 * 1024
        ),
        cost_estimate=SMALL,
    )(*ops)


def attn_back_kernel(
    d_hidden, q, mixed, kv, wo_a, wo_b, cos, sin, seg_q, seg_k,
    d_out, d_q, d_kv, bias, wo, grad,
):
    j = pl.program_id(0)
    rows = grad.shape[0]
    before = kv.shape[0] - rows

    @pl.when(j == 0)
    def _():
        grad[...] = d_hidden[...].astype(BF16)
        d_kv[...] = jnp.zeros_like(d_kv)
        put_bias(seg_q, seg_k, bias)

    take(j, wo_a, wo_b, wo)
    d_out[0] = t_mm(mixed[0], grad[...]).astype(BF16)
    for at in range(0, rows, BLOCK):
        here = pl.ds(at, BLOCK)
        keys = pl.ds(at, before + BLOCK)
        q_here = q[0, here, :]
        d_mixed = mm_t(grad[here, :], wo[...]).astype(BF16)
        probs = softmax(mm_t(q_here, kv[keys, :HD]) + bias[here, keys])
        d_probs = mm_t(d_mixed, kv[keys, HD:])
        inner = jnp.sum(probs * d_probs, axis=-1, keepdims=True)
        d_scores = (probs * (d_probs - inner)).astype(BF16)
        back = unrotate(mm(d_scores, kv[keys, :HD]), cos[here, :], sin[here, :]) * HD**-0.5
        d_q[0, here, :] = back.astype(BF16)
        d_kv[keys, :HD] += t_mm(d_scores, q_here)
        d_kv[keys, HD:] += t_mm(probs.astype(BF16), d_mixed)


def attn_back(d_hidden, q, mixed, kv, w, place):
    cos, sin, seg_q, seg_k = place
    rows, width = d_hidden.shape
    total = kv.shape[0]
    cos, sin = cos[total - rows :], sin[total - rows :]
    ops = (d_hidden, q, mixed, kv, *w["out"], cos, sin, seg_q, seg_k)
    pairs = {1: step_of, 2: step_of, 4: first_of, 5: last_of}
    outs = (STEPS, HD, width)
    return pl.pallas_call(
        attn_back_kernel,
        out_shape=(
            jax.ShapeDtypeStruct(outs, BF16),
            jax.ShapeDtypeStruct(q.shape, BF16),
            jax.ShapeDtypeStruct((total, 2 * HD), F32),
        ),
        in_specs=[pairs.get(i, all_of)(op.shape) for i, op in enumerate(ops)],
        out_specs=(step_of(outs), step_of(q.shape), all_of((total, 2 * HD))),
        scratch_shapes=[
            pltpu.VMEM((rows, total), F32),
            pltpu.VMEM((HD, width), BF16),
            pltpu.VMEM((rows, width), BF16),
        ],
        cost_estimate=SMALL,
        **PARAMS,
    )(*ops)


def query_back_kernel(d_q, normed, wq_a, wq_b, d_query, d_normed, wq):
    j = pl.program_id(0)
    take(j, wq_a, wq_b, wq)
    d_query[0] = t_mm(d_q[0], normed[...]).astype(BF16)
    term = mm_t(d_q[0], wq[...])

    @pl.when(j == 0)
    def _():
        d_normed[...] = term

    @pl.when(j > 0)
    def _():
        d_normed[...] += term


def query_back(d_q, normed, w):
    rows, width = normed.shape
    ops = (d_q, normed, *w["query"])
    outs = (STEPS, HD, width)
    pairs = {0: step_of, 2: first_of, 3: last_of}
    return pl.pallas_call(
        query_back_kernel,
        out_shape=(jax.ShapeDtypeStruct(outs, BF16), jax.ShapeDtypeStruct((rows, width), F32)),
        in_specs=[pairs.get(i, all_of)(op.shape) for i, op in enumerate(ops)],
        out_specs=(step_of(outs), all_of((rows, width))),
        scratch_shapes=[pltpu.VMEM((width, HD), BF16)],
        cost_estimate=SMALL,
        **PARAMS,
    )(*ops)


def input_back_kernel(
    d_kv, behind, normed, wk, wv, d_normed, x_ref, gain, d_hidden, cos, sin, d_x, d_shared, d_gain
):
    total = d_kv[...] + behind[...].astype(F32)
    d_k = unrotate(total[:, :HD], cos[...], sin[...]).astype(BF16)
    d_v = total[:, HD:].astype(BF16)
    d_shared[:HD, :] = t_mm(d_k, normed[...]).astype(BF16)
    d_shared[HD:, :] = t_mm(d_v, normed[...]).astype(BF16)
    grad = d_normed[...] + mm_t(d_k, wk[...]) + mm_t(d_v, wv[...])
    to_x, to_gain = norm_back(x_ref[...].astype(F32), gain[...], grad)
    d_x[...] = (d_hidden[...] + to_x).astype(BF16)
    d_gain[...] = to_gain[None]


def input_back(d_kv, behind, normed, d_normed, x, d_hidden, w, place):
    cos, sin = place[:2]
    rows, width = normed.shape
    before = cos.shape[0] - rows
    ops = (
        d_kv[before:], behind, normed, w["key"], w["value"], d_normed, x, w["gain_attn"], d_hidden,
        cos[before:], sin[before:],
    )
    return pl.pallas_call(
        input_back_kernel,
        out_shape=(
            jax.ShapeDtypeStruct((rows, width), BF16),
            jax.ShapeDtypeStruct((2 * HD, width), BF16),
            jax.ShapeDtypeStruct((1, width), F32),
        ),
        compiler_params=pltpu.CompilerParams(vmem_limit_bytes=56 * 1024 * 1024),
        cost_estimate=SMALL,
    )(*ops)


def pack_attn(d_query, d_out, d_shared, d_gain_attn, d_gain_ff, order):
    gains = jnp.concatenate([d_gain_attn, d_gain_ff])
    gains = jnp.pad(gains, ((0, GAIN_ROWS - 2), (0, 0))).astype(BF16)
    count = d_shared.shape[0] // STEPS
    pieces = []
    for j in range(STEPS):
        quarter = lax.dynamic_slice_in_dim(d_shared, (order ^ j) * count, count, 0)
        pieces.append(jnp.concatenate([d_query[j], d_out[j], quarter, gains]))
    return jnp.stack(pieces[:2]), jnp.stack(pieces[2:])


def finish_part(scale, source, at, size):
    return source[at : at + size, :].astype(F32) * scale


def for_core(core, put, mine, other):
    @pl.when(core[0] == 0)
    def _():
        put(0, *mine)
        put(1, *other)

    @pl.when(core[0] != 0)
    def _():
        put(0, *other)
        put(1, *mine)


def finish_ffn_kernel(scale, core, *refs):
    gate, up, down = refs[4:]
    units = gate.shape[1] // 2
    part = functools.partial(finish_part, scale)

    def put(core, low, high):
        at = core * units
        gate[:, at : at + units // 2] = part(low, 0, units // 2).T
        gate[:, at + units // 2 : at + units] = part(high, 0, units // 2).T
        up[:, at : at + units] = part(low, units // 2, units).T
        down[at : at + units, :] = part(high, units // 2, units)

    for_core(core, put, refs[:2], refs[2:4])


def finish_attn_kernel(scale, core, *refs):
    shared = refs[4]
    query, key, value, out = refs[5:]
    heads = query.shape[1] // 2
    part = functools.partial(finish_part, scale)

    def put(core, low, high):
        some, at = low.shape[0] - heads, core * heads
        query[:, at : at + heads] = part(low, 0, heads).T
        out[at : at + some, :] = part(low, heads, some)
        out[at + some : at + heads, :] = part(high, 0, heads - some)

    for_core(core, put, refs[:2], refs[2:4])
    key[...] = part(shared, 0, HD).T
    value[...] = part(shared, HD, HD).T


def finish(kernel, shapes, core, scale, *ops):
    vmem = pl.BlockSpec(memory_space=pltpu.VMEM)
    return pl.pallas_call(
        functools.partial(kernel, scale),
        out_shape=[jax.ShapeDtypeStruct(shape, F32) for shape in shapes],
        in_specs=[pl.BlockSpec(memory_space=pltpu.SMEM)] + [vmem] * len(ops),
        out_specs=[vmem] * len(shapes),
        compiler_params=pltpu.CompilerParams(vmem_limit_bytes=56 * 1024 * 1024),
        cost_estimate=SMALL,
    )(core.reshape(1), *ops)


def finish_ffn(mine, other, core, scale, units):
    width = mine[0].shape[1]
    shapes = [(width, units), (width, units), (units, width)]
    return finish(finish_ffn_kernel, shapes, core, scale, *mine, *other)


def finish_attn(mine, other, shared, core, scale, heads):
    width = shared.shape[1]
    shapes = [(width, heads), (width, HD), (width, HD), (heads, width)]
    return finish(finish_attn_kernel, shapes, core, scale, *mine, *other, shared)


def halves(total, section, axis):
    half = total.shape[axis] // 2
    low, high = (lax.slice_in_dim(total, i * half, (i + 1) * half, axis=axis) for i in range(2))
    return pick(section == 0, low, high), pick(section == 0, high, low)


def to_owner(value, layer):
    return lax.ppermute(value, "section", [(1 - layer, layer)])


def local(
    x_input,
    doc_lengths,
    cotangent,
    gain_attn,
    w_query,
    w_key,
    w_value,
    w_out,
    gain_ff,
    w_gate,
    w_up,
    w_down,
):
    section = lax.axis_index("section")
    gx, gy = lax.axis_index("gx"), lax.axis_index("gy")
    own_rows = x_input.shape[2]
    scale = 1.0 / lax.axis_size("dp")

    def mine(value):
        return lax.dynamic_index_in_dim(value[:, 0], section, 0, keepdims=False)

    x = mine(x_input)
    first, x_before, finish_weights = gather_weights(
        x, w_query[0], w_key[0], w_value[0], w_out[0], w_gate[0], w_up[0], w_down[0], section
    )
    gains = jnp.concatenate([gain_attn, gain_ff])
    other_gains = swap(gains, "section")
    gains = [pick(section == layer, gains, other_gains) for layer in range(2)]
    first.update(gain_attn=gains[0][:1], gain_ff=gains[0][1:])

    x_all = jnp.concatenate([x_before, x])
    start = (gx * lax.axis_size("gy") + gy) * own_rows
    rows = start - WINDOW + jnp.arange(WINDOW + own_rows, dtype=jnp.int32)
    segment, where_in, valid = layout(mine(doc_lengths), rows)
    frequency = jnp.exp(jnp.arange(HD // 2, dtype=F32) * (-2.0 * math.log(10000.0) / HD))
    angles = where_in.astype(F32)[:, None] * frequency[None, :]
    place = (jnp.cos(angles), jnp.sin(angles), segment[WINDOW:, None], segment[None, :])

    q_0, mixed_0, kv_0, normed_0, hidden_0 = attn_forward(x_all, first, place)
    hidden_0, second = finish_weights(hidden_0)
    out_0 = ffn_forward(hidden_0, first)
    out_0, rows_before, second = second(out_0)
    second.update(gain_attn=gains[1][:1], gain_ff=gains[1][1:])
    out_all = jnp.concatenate([rows_before, out_0])
    slot = lambda *values: lax.optimization_barrier(values)
    q_1, mixed_1, kv_1, normed_1, hidden_1 = attn_forward(out_all, second, place)
    out_0_other = lax.ppermute(out_0, "section", [(1, 0)])
    hidden_1, out_0_other, up_1 = slot(hidden_1, out_0_other, second["up"])
    up_1 = jnp.stack(up_1)
    second.update(up=(up_1, swap(up_1, "gx")))

    order = 2 * gx + gy
    dy = jnp.where(valid[WINDOW:, None], mine(cotangent), 0)
    turn = w_gate.shape[2] // 2

    def ffn_parts(near, got):
        a_near, a_far = (near[i, :turn] + got[i, :turn] for i in range(2))
        return a_near, a_far, near[:, turn:] + got[:, turn:]

    far, before = ffn_back(dy, hidden_1, second, 1)
    before, far = slot(before, far)
    got = swap(far, "gx")
    near, d_hidden, gain_ff = ffn_back(dy, hidden_1, second, 0, before)
    near, d_hidden, gain_ff, got = slot(near, d_hidden, gain_ff, got)
    a_near, a_far, b = ffn_parts(near, got)
    b_keep, b_send = halves(b, section, 1)
    a_got = swap(a_far, "gy")
    b_got = swap(b_send, "section")
    out_1 = ffn_forward(hidden_1, second)
    d_out, d_q, d_kv = attn_back(d_hidden, q_1, mixed_1, kv_1, second, place)
    d_q, d_kv, out_1, a_got, b_got = slot(d_q, d_kv, out_1, a_got, b_got)
    sent = d_kv[:WINDOW].astype(BF16)
    a_keep, a_send = halves(a_near + a_got, section, 0)
    b = b_keep + b_got
    behind = to_before(sent)
    a_got = swap(a_send, "section")
    d_query, d_normed = query_back(d_q, normed_1, second)
    d_normed, behind, b, a_got = slot(d_normed, behind, b, a_got)
    b_far = swap(b[1], "gy")
    grad_1, d_shared, gain_attn_grad = input_back(
        d_kv, behind, normed_1, d_normed, out_0, d_hidden, second, place
    )
    near, far = pack_attn(d_query, d_out, d_shared, gain_attn_grad, gain_ff, order)
    got = swap(far, "gx")
    grad_1, near, got = slot(grad_1, near, got)

    c_keep_1, c_send_1 = halves(near + got, section, 1)
    c_send_a, c_send_b = c_send_1[0], c_send_1[1]
    c_got_a = swap(c_send_a, "section")
    far, before = ffn_back(grad_1, hidden_0, first, 1)
    before, far, b_far, c_got_a = slot(before, far, b_far, c_got_a)
    ffn_1 = jnp.concatenate([a_keep + a_got, b[0] + b_far])
    got = swap(far, "gx")
    c_got_b = swap(c_send_b, "section")
    near, d_hidden, gain_ff = ffn_back(grad_1, hidden_0, first, 0, before)
    near, d_hidden, gain_ff, got, c_got_b = slot(near, d_hidden, gain_ff, got, c_got_b)
    a_near, a_far, b = ffn_parts(near, got)
    b_keep, b_send = halves(b, section, 1)
    b_got = swap(b_send, "section")
    a_got = swap(a_far, "gy")
    d_out, d_q, d_kv = attn_back(d_hidden, q_0, mixed_0, kv_0, first, place)
    c_1 = [c_keep_1[0] + c_got_a, c_keep_1[1] + c_got_b]
    d_q, d_kv, a_got = slot(d_q, d_kv, a_got)
    sent = d_kv[:WINDOW].astype(BF16)
    a_keep, a_send = halves(a_near + a_got, section, 0)
    behind = to_before(sent)
    a_got = swap(a_send, "section")
    d_query, d_normed = query_back(d_q, normed_0, first)
    d_normed, behind, b_got, a_got = slot(d_normed, behind, b_got, a_got)
    b = b_keep + b_got
    b_far = swap(b[1], "gy")
    grad_0, d_shared, gain_attn_grad = input_back(
        d_kv, behind, normed_0, d_normed, x, d_hidden, first, place
    )
    near, far = pack_attn(d_query, d_out, d_shared, gain_attn_grad, gain_ff, order)
    got = swap(far, "gx")
    near, got, b_far = slot(near, got, b_far)
    count = ffn_1.shape[0]
    ffn = lax.psum(jnp.concatenate([ffn_1, a_keep + a_got, b[0] + b_far]), "dp")
    c_keep, c_send = halves(near + got, section, 1)
    c_got = swap(c_send, "section")
    c_far_1 = swap(c_1[1], "gy")
    c_keep, c_got, c_far_1 = slot(c_keep, c_got, c_far_1)
    c = c_keep + c_got
    c_far = swap(c[1], "gy")
    grad_other = swap(pick(section == 0, grad_1, grad_0), "section")
    out_1_other = lax.ppermute(out_1, "section", [(0, 1)])
    ffn, c_far, grad_other, out_1_other = slot(ffn, c_far, grad_other, out_1_other)
    attn = jnp.concatenate([c_1[0] + c_far_1, c[0] + c_far])
    half = ffn.shape[0] // 2
    sent = pick(section == 0, ffn[:half], ffn[half:])
    ffn_got = swap(sent, "section")
    attn = lax.psum(attn, "dp")
    attn, ffn_got = slot(attn, ffn_got)

    def two_halves(both, got):
        half = both.shape[0] // 2
        mine = pick(section == 0, both[half:], both[:half])
        return pick(section == 0, mine, got), pick(section == 0, got, mine)

    half = attn.shape[0] // 2
    attn_got = swap(pick(section == 0, attn[:half], attn[half:]), "section")
    ffn_mine = two_halves(ffn, ffn_got)
    gate, up, down = finish_ffn(
        ffn_mine, [swap(value, "gx") for value in ffn_mine], gx, scale, w_gate.shape[2]
    )
    states, in_grads = pick(section == 0, out_0, out_1), pick(section == 0, grad_0, grad_1)
    other_states = pick(section == 0, out_0_other, out_1_other)

    def by_micro(own, other):
        first = section == 0
        return jnp.stack([jnp.where(first, own, other), jnp.where(first, other, own)])[
            None, :, None
        ]

    states, in_grads = by_micro(states, other_states), by_micro(in_grads, grad_other)
    attn_got, gate, up, down, states, in_grads = slot(attn_got, gate, up, down, states, in_grads)
    attn_low, high = two_halves(attn, attn_got)
    attn_others = swap(attn_low, "gx"), swap(high, "gx")
    count = d_shared.shape[0] // STEPS
    quarter = high[-GAIN_ROWS - count : -GAIN_ROWS]
    gain_sums = high[-GAIN_ROWS : 2 - GAIN_ROWS].astype(F32) * scale
    beside = swap(quarter, "gy")
    both = pick(
        gy == 0, jnp.concatenate([quarter, beside]), jnp.concatenate([beside, quarter])
    )
    both_other = swap(both, "gx")
    shared = pick(
        gx == 0, jnp.concatenate([both, both_other]), jnp.concatenate([both_other, both])
    )
    query, key, value, out = finish_attn(
        (attn_low, high), attn_others, shared, gx, scale, w_query.shape[2]
    )

    return (
        states,
        in_grads,
        gain_sums[:1],
        query[None],
        key[None],
        value[None],
        out[None],
        gain_sums[1:],
        gate[None],
        up[None],
        down[None],
    )


def solution(mesh):
    rows = P(None, "dp", ("gx", "gy"), None)
    columns = P("section", None, "gy")
    depth = P("section", "gy", None)
    whole = P("section", None, None)
    gain = P("section", None)
    by_layer = P("section", None, "dp", ("gx", "gy"), None)
    return jax.shard_map(
        local,
        mesh=mesh,
        in_specs=(
            rows,
            P(None, "dp", None),
            rows,
            gain,
            columns,
            whole,
            whole,
            depth,
            gain,
            columns,
            columns,
            depth,
        ),
        out_specs=(
            by_layer,
            by_layer,
            gain,
            columns,
            whole,
            whole,
            depth,
            gain,
            columns,
            columns,
            depth,
        ),
        check_vma=False,
    )
```

```python
import functools
import math

import jax
import jax.numpy as jnp
from jax import lax
from jax.experimental import pallas as pl
from jax.experimental.pallas import tpu as pltpu
from jax.sharding import PartitionSpec as P

HD = 256
WINDOW = 512
GAIN_ROWS = 32
F32 = jnp.float32
BF16 = jnp.bfloat16


def swap(value, axis):
    return lax.ppermute(value, axis, [(0, 1), (1, 0)])


def mm(a, b):
    return jnp.dot(a, b, preferred_element_type=F32)


def mm_t(a, b):
    return lax.dot_general(a, b, (((1,), (1,)), ((), ())), preferred_element_type=F32)


def t_mm(a, b):
    return lax.dot_general(a, b, (((0,), (0,)), ((), ())), preferred_element_type=F32)


def inverse_rms(value):
    return lax.rsqrt(jnp.mean(value * value, axis=-1, keepdims=True) + 1e-06)


def norm_back(value, gain, grad):
    s = inverse_rms(value)
    scaled = grad * gain
    to_value = s * scaled - value * (s * s * s) * jnp.mean(value * scaled, axis=-1, keepdims=True)
    return to_value, jnp.sum(grad * value * s, axis=0)


def rotate(value, cos, sin):
    half = value.shape[-1] // 2
    a, b = value[..., :half], value[..., half:]
    return jnp.concatenate([a * cos - b * sin, b * cos + a * sin], axis=-1)


def unrotate(value, cos, sin):
    half = value.shape[-1] // 2
    c, e = value[..., :half], value[..., half:]
    return jnp.concatenate([c * cos + e * sin, e * cos - c * sin], axis=-1)


def gelu_parts(v):
    c = math.sqrt(2.0 / math.pi)
    t = jnp.tanh(c * (v + 0.044715 * v * v * v))
    value = 0.5 * v * (1.0 + t)
    slope = 0.5 * (1.0 + t) + 0.5 * v * (1.0 - t * t) * (c * (1.0 + 3 * 0.044715 * v * v))
    return value, slope


def layout(lengths, rows):
    docs = lengths.shape[0]
    ends = jnp.cumsum(lengths)
    number = jnp.sum((rows[:, None] >= ends[None, :]).astype(jnp.int32), axis=1)
    valid = number < docs
    begin = jnp.sum(
        jnp.where(number[:, None] == jnp.arange(docs)[None, :], (ends - lengths)[None, :], 0), axis=1
    )
    place = jnp.where(valid, rows - begin, 0)
    segment = jnp.where(rows < 0, -1, jnp.where(valid, number, docs + rows))
    return segment, place, valid


def pick(flag, a, b):
    return jnp.where(flag, a, b)


def gather_weights(x, w_query, w_key, w_value, w_out, w_gate, w_up, w_down, section):
    gx = lax.axis_index("gx")
    barrier = lax.optimization_barrier

    def half(w, axis):
        size = w.shape[axis] // 2
        return lax.dynamic_slice_in_dim(w, gx * size, size, axis)

    def two_layers(mine, received):
        return [pick(section == layer, mine, received) for layer in range(2)]

    def over_gx(own, beside):
        both = jnp.stack([own, beside])
        return both, swap(both, "gx")

    heads = w_query.shape[1] // 2
    first_own = jnp.concatenate([half(w_query, 1), half(w_key, 1), half(w_value, 1)], axis=1)
    out_own, gate_own, up_own, down_own = half(w_out, 0), half(w_gate, 1), half(w_up, 1), half(w_down, 0)
    first_got = swap(first_own, "section")
    x_before = from_before(x)
    out_got = swap(out_own, "section")
    down_beside = swap(down_own, "gy")
    first_got, gate_own = barrier((first_got, gate_own))

    queries = two_layers(first_own[:, :heads], first_got[:, :heads])
    query_beside = swap(queries[0], "gy")
    gate_got = swap(gate_own, "section")
    shared_got = first_got[:, heads:]
    shared_other = swap(shared_got, "gx")
    out_got, up_own = barrier((out_got, up_own))

    outs = two_layers(out_own, out_got)
    out_beside = swap(outs[0], "gy")
    up_got = swap(up_own, "section")
    low, high = pick(gx == 0, shared_got, shared_other), pick(gx == 0, shared_other, shared_got)
    part = low.shape[1] // 2
    key_got = jnp.concatenate([low[:, :part], high[:, :part]], axis=1)
    value_got = jnp.concatenate([low[:, part:], high[:, part:]], axis=1)
    keys, values = two_layers(w_key, key_got), two_layers(w_value, value_got)
    down_pair = jnp.stack([down_own, down_beside])
    gate_got, down_pair, keys, values = barrier((gate_got, down_pair, keys, values))

    gates = two_layers(gate_own, gate_got)
    gate_beside = swap(gates[0], "gy")
    down_got = swap(down_pair, "section")
    query_beside, out_beside, x_before, up_got = barrier((query_beside, out_beside, x_before, up_got))
    ups = two_layers(up_own, up_got)
    up_beside = swap(ups[0], "gy")
    later = queries[1], outs[1]
    later_besides = [swap(value, "gy") for value in later]
    first = {
        "query": over_gx(queries[0], query_beside),
        "out": over_gx(outs[0], out_beside),
        "key": keys[0],
        "value": values[0],
    }

    def finish(kernel_out):
        kernel_out, gate_here, up_here, arrived, gate_1 = barrier(
            (kernel_out, gate_beside, up_beside, later_besides, gates[1])
        )
        gate_1_beside = swap(gate_1, "gy")
        downs = two_layers(down_pair, down_got)
        first.update(
            gate=over_gx(gates[0], gate_here),
            up=over_gx(ups[0], up_here),
            down=(downs[0], swap(downs[0], "gx")),
        )

        def second(kernel_out):
            kernel_out, gate_1_here, up_1, down_1 = barrier(
                (kernel_out, gate_1_beside, ups[1], downs[1])
            )
            rows_before = from_before(kernel_out)
            down_pairs = down_1, swap(down_1, "gx")
            query_pairs, out_pairs = over_gx(later[0], arrived[0]), over_gx(later[1], arrived[1])
            gate_pairs = over_gx(gate_1, gate_1_here)
            rows_before, up_1, gate_pairs, down_pairs, query_pairs, out_pairs = barrier(
                (rows_before, up_1, gate_pairs, down_pairs, query_pairs, out_pairs)
            )
            layer = {
                "query": query_pairs,
                "out": out_pairs,
                "gate": gate_pairs,
                "up": (up_1, swap(up_1, "gy")),
                "down": down_pairs,
                "key": keys[1],
                "value": values[1],
            }
            return kernel_out, rows_before, layer

        return kernel_out, second

    return first, x_before, finish


def from_before(value):
    return lax.ppermute(value, ("gx", "gy"), [(0, 1), (1, 2), (2, 3)])


def to_before(value):
    return lax.ppermute(value, ("gx", "gy"), [(1, 0), (2, 1), (3, 2)])


BLOCK = 256
STEPS = 4
PARAMS = dict(
    grid=(STEPS,),
    compiler_params=pltpu.CompilerParams(
        dimension_semantics=("arbitrary",), vmem_limit_bytes=56 * 1024 * 1024
    ),
)


def all_of(shape):
    return pl.BlockSpec(shape, lambda j: (0,) * len(shape))


def step_of(shape):
    return pl.BlockSpec((1,) + shape[1:], lambda j: (j,) + (0,) * (len(shape) - 1))


def first_of(shape):
    return pl.BlockSpec((1,) + shape[1:], lambda j: (jnp.minimum(j, 1),) + (0,) * (len(shape) - 1))


def last_of(shape):
    return pl.BlockSpec(
        (1,) + shape[1:], lambda j: (jnp.maximum(j - 2, 0),) + (0,) * (len(shape) - 1)
    )


SMALL = pl.CostEstimate(flops=1000, bytes_accessed=1000, transcendentals=0)


def take(step, first, last, held):
    @pl.when(step < 2)
    def _():
        held[...] = first[0]

    @pl.when(step >= 2)
    def _():
        held[...] = last[0]


def put_bias(seg_q, seg_k, bias):
    rows, keys = bias.shape
    distance = (
        lax.broadcasted_iota(jnp.int32, (rows, keys), 0)
        + (keys - rows)
        - lax.broadcasted_iota(jnp.int32, (rows, keys), 1)
    )
    allowed = (distance >= 0) & (distance < WINDOW) & (seg_q[...] == seg_k[...])
    bias[...] = jnp.where(allowed, 0.0, -1e30)


def softmax(scores):
    weights = jnp.exp(scores - jnp.max(scores, axis=-1, keepdims=True))
    return weights * (1.0 / jnp.sum(weights, axis=-1, keepdims=True))


def attn_kernel(
    x_ref, gain, wq_a, wq_b, wk, wv, wo_a, wo_b, cos, sin, seg_q, seg_k,
    q_out, mixed_out, kv_out, normed_out, hidden_out, bias, wq, wo,
):
    j = pl.program_id(0)
    rows = normed_out.shape[0]
    before = x_ref.shape[0] - rows

    @pl.when(j == 0)
    def _():
        x = x_ref[...].astype(F32)
        normed = (x * inverse_rms(x) * gain[...]).astype(BF16)
        normed_out[...] = normed[before:]
        kv_out[:, :HD] = rotate(mm(normed, wk[...]), cos[...], sin[...]).astype(BF16)
        kv_out[:, HD:] = mm(normed, wv[...]).astype(BF16)
        hidden_out[...] = x[before:]
        put_bias(seg_q, seg_k, bias)

    take(j, wq_a, wq_b, wq)
    take(j, wo_a, wo_b, wo)
    q = rotate(mm(normed_out[...], wq[...]), cos[before:, :], sin[before:, :]) * HD**-0.5
    q_out[0] = q.astype(BF16)
    for at in range(0, rows, BLOCK):
        here = pl.ds(at, BLOCK)
        keys = pl.ds(at, before + BLOCK)
        scores = mm_t(q_out[0, here, :], kv_out[keys, :HD]) + bias[here, keys]
        mixed = mm(softmax(scores).astype(BF16), kv_out[keys, HD:]).astype(BF16)
        mixed_out[0, here, :] = mixed
        hidden_out[here, :] += mm(mixed, wo[...])


def attn_forward(x_all, w, place):
    cos, sin, seg_q, seg_k = place
    total, width = x_all.shape
    rows = seg_q.shape[0]
    heads = (STEPS, rows, HD)
    ops = (x_all, w["gain_attn"], *w["query"], w["key"], w["value"], *w["out"], cos, sin, seg_q, seg_k)
    pairs = {2: first_of, 3: last_of, 6: first_of, 7: last_of}
    return pl.pallas_call(
        attn_kernel,
        out_shape=(
            jax.ShapeDtypeStruct(heads, BF16),
            jax.ShapeDtypeStruct(heads, BF16),
            jax.ShapeDtypeStruct((total, 2 * HD), BF16),
            jax.ShapeDtypeStruct((rows, width), BF16),
            jax.ShapeDtypeStruct((rows, width), F32),
        ),
        in_specs=[pairs.get(i, all_of)(op.shape) for i, op in enumerate(ops)],
        out_specs=(
            step_of(heads),
            step_of(heads),
            all_of((total, 2 * HD)),
            all_of((rows, width)),
            all_of((rows, width)),
        ),
        scratch_shapes=[
            pltpu.VMEM((rows, total), F32),
            pltpu.VMEM((width, HD), BF16),
            pltpu.VMEM((HD, width), BF16),
        ],
        cost_estimate=SMALL,
        **PARAMS,
    )(*ops)


def ffn_kernel(
    hidden, gain, gate_a, gate_b, up_a, up_b, down_a, down_b,
    out, normed, total, w_gate, w_up, down,
):
    j = pl.program_id(0)

    @pl.when(j == 0)
    def _():
        value = hidden[...]
        normed[...] = (value * inverse_rms(value) * gain[...]).astype(BF16)
        total[...] = value

    take(j, gate_a, gate_b, w_gate)
    take(j, up_a, up_b, w_up)
    take(j, down_a, down_b, down)
    gate = mm(normed[...], w_gate[...])
    up = mm(normed[...], w_up[...])
    act = (gelu_parts(gate)[0] * up).astype(BF16)
    total[...] += mm(act, down[...])

    @pl.when(j == STEPS - 1)
    def _():
        out[...] = total[...].astype(BF16)


def ffn_forward(hidden, w):
    rows, width = hidden.shape
    ops = (hidden, w["gain_ff"], *w["gate"], *w["up"], *w["down"])
    units = w["down"][0].shape[1]
    pairs = {i: (first_of, last_of)[i % 2] for i in range(2, 8)}
    return pl.pallas_call(
        ffn_kernel,
        out_shape=jax.ShapeDtypeStruct((rows, width), BF16),
        in_specs=[pairs.get(i, all_of)(op.shape) for i, op in enumerate(ops)],
        out_specs=all_of((rows, width)),
        scratch_shapes=[
            pltpu.VMEM((rows, width), BF16),
            pltpu.VMEM((rows, width), F32),
            pltpu.VMEM((width, units), BF16),
            pltpu.VMEM((width, units), BF16),
            pltpu.VMEM((units, width), BF16),
        ],
        cost_estimate=SMALL,
        **PARAMS,
    )(*ops)


def ffn_back_kernel(last, dy, hidden, gain, before, gate, up, down, out, *rest):
    total, normed = rest[-2:]
    j = pl.program_id(0)
    units = down.shape[1]

    @pl.when(j == 0)
    def _():
        value = hidden[...]
        normed[...] = (value * inverse_rms(value) * gain[...]).astype(BF16)
        total[...] = before[...] if last else jnp.zeros_like(total)

    gate_value = mm(normed[...], gate[0])
    up_value = mm(normed[...], up[0])
    d_act = mm_t(dy[...], down[0])
    value, slope = gelu_parts(gate_value)
    act = (value * up_value).astype(BF16)
    d_gate = (d_act * up_value * slope).astype(BF16)
    d_up = (d_act * value).astype(BF16)
    total[...] += mm_t(d_gate, gate[0]) + mm_t(d_up, up[0])
    for i, part in enumerate((t_mm(d_gate, normed[...]), t_mm(d_up, normed[...]), t_mm(act, dy[...]))):
        out[0, pl.ds(i * units, units), :] = part.astype(BF16)

    @pl.when(j == pl.num_programs(0) - 1)
    def _():
        if last:
            d_hidden, d_gain = rest[:2]
            to_hidden, to_gain = norm_back(hidden[...], gain[...], total[...])
            d_hidden[...] = dy[...].astype(F32) + to_hidden
            d_gain[...] = to_gain[None]
        else:
            rest[0][...] = total[...]


def ffn_back(dy, hidden, w, pair, before=None):
    rows, width = hidden.shape
    last = before is not None
    ops = (dy, hidden, w["gain_ff"], before if last else jnp.zeros((8, 128), F32))
    ops += (w["gate"][pair], w["up"][pair], w["down"][pair])
    packed = (2, 3 * w["down"][pair].shape[1], width)
    shapes = [(rows, width), (1, width)] if last else [(rows, width)]
    return pl.pallas_call(
        functools.partial(ffn_back_kernel, last),
        grid=(2,),
        out_shape=[jax.ShapeDtypeStruct(packed, BF16)]
        + [jax.ShapeDtypeStruct(shape, F32) for shape in shapes],
        in_specs=[all_of(op.shape) for op in ops[:4]] + [step_of(op.shape) for op in ops[4:]],
        out_specs=[step_of(packed)] + [all_of(shape) for shape in shapes],
        scratch_shapes=[pltpu.VMEM((rows, width), F32), pltpu.VMEM((rows, width), BF16)],
        compiler_params=pltpu.CompilerParams(
            dimension_semantics=("arbitrary",), vmem_limit_bytes=56 * 1024 * 1024
        ),
        cost_estimate=SMALL,
    )(*ops)


def put_pair(step, near, far, value):
    @pl.when(step < 2)
    def _():
        near[0] = value

    @pl.when(step >= 2)
    def _():
        far[0] = value


def attn_back_kernel(
    d_hidden, q, mixed, kv, wo_a, wo_b, cos, sin, seg_q, seg_k,
    near, far, d_q, sent, own, bias, wo, grad, d_kv,
):
    j = pl.program_id(0)
    rows = grad.shape[0]
    before = kv.shape[0] - rows

    @pl.when(j == 0)
    def _():
        grad[...] = d_hidden[...].astype(BF16)
        d_kv[...] = jnp.zeros_like(d_kv)
        put_bias(seg_q, seg_k, bias)

    take(j, wo_a, wo_b, wo)
    put_pair(j, near, far, t_mm(mixed[0], grad[...]).astype(BF16))
    for at in range(0, rows, BLOCK):
        here = pl.ds(at, BLOCK)
        place = pl.ds(before + at, BLOCK)
        keys = pl.ds(at, before + BLOCK)
        q_here = q[0, here, :]
        d_mixed = mm_t(grad[here, :], wo[...]).astype(BF16)
        probs = softmax(mm_t(q_here, kv[keys, :HD]) + bias[here, keys])
        d_probs = mm_t(d_mixed, kv[keys, HD:])
        inner = jnp.sum(probs * d_probs, axis=-1, keepdims=True)
        d_scores = (probs * (d_probs - inner)).astype(BF16)
        back = unrotate(mm(d_scores, kv[keys, :HD]), cos[place, :], sin[place, :]) * HD**-0.5
        d_q[0, here, :] = back.astype(BF16)
        d_kv[keys, :HD] += t_mm(d_scores, q_here)
        d_kv[keys, HD:] += t_mm(probs.astype(BF16), d_mixed)

    @pl.when(j == STEPS - 1)
    def _():
        sent[...] = d_kv[:before, :].astype(BF16)
        own[...] = d_kv[before:, :]


def attn_back(d_hidden, q, mixed, kv, w, place):
    rows, width = d_hidden.shape
    total = kv.shape[0]
    ops = (d_hidden, q, mixed, kv, *w["out"], *place)
    pairs = {1: step_of, 2: step_of, 4: first_of, 5: last_of}
    outs = (2, HD, width)
    return pl.pallas_call(
        attn_back_kernel,
        out_shape=(
            jax.ShapeDtypeStruct(outs, BF16),
            jax.ShapeDtypeStruct(outs, BF16),
            jax.ShapeDtypeStruct(q.shape, BF16),
            jax.ShapeDtypeStruct((total - rows, 2 * HD), BF16),
            jax.ShapeDtypeStruct((rows, 2 * HD), F32),
        ),
        in_specs=[pairs.get(i, all_of)(op.shape) for i, op in enumerate(ops)],
        out_specs=(
            first_of(outs),
            last_of(outs),
            step_of(q.shape),
            all_of((total - rows, 2 * HD)),
            all_of((rows, 2 * HD)),
        ),
        scratch_shapes=[
            pltpu.VMEM((rows, total), F32),
            pltpu.VMEM((HD, width), BF16),
            pltpu.VMEM((rows, width), BF16),
            pltpu.VMEM((total, 2 * HD), F32),
        ],
        cost_estimate=SMALL,
        **PARAMS,
    )(*ops)


def query_back_kernel(d_q, normed, wq_a, wq_b, near, far, d_normed, wq):
    j = pl.program_id(0)
    take(j, wq_a, wq_b, wq)
    put_pair(j, near, far, t_mm(d_q[0], normed[...]).astype(BF16))
    term = mm_t(d_q[0], wq[...])

    @pl.when(j == 0)
    def _():
        d_normed[...] = term

    @pl.when(j > 0)
    def _():
        d_normed[...] += term


def query_back(d_q, normed, w):
    rows, width = normed.shape
    ops = (d_q, normed, *w["query"])
    outs = (2, HD, width)
    pairs = {0: step_of, 2: first_of, 3: last_of}
    return pl.pallas_call(
        query_back_kernel,
        out_shape=(
            jax.ShapeDtypeStruct(outs, BF16),
            jax.ShapeDtypeStruct(outs, BF16),
            jax.ShapeDtypeStruct((rows, width), F32),
        ),
        in_specs=[pairs.get(i, all_of)(op.shape) for i, op in enumerate(ops)],
        out_specs=(first_of(outs), last_of(outs), all_of((rows, width))),
        scratch_shapes=[pltpu.VMEM((width, HD), BF16)],
        cost_estimate=SMALL,
        **PARAMS,
    )(*ops)


def input_back_kernel(
    d_kv, behind, normed, wk, wv, d_normed, x_ref, gain, d_hidden, cos, sin, d_x, d_shared, d_gain
):
    before = cos.shape[0] - normed.shape[0]
    total = d_kv[...] + behind[...].astype(F32)
    d_k = unrotate(total[:, :HD], cos[before:, :], sin[before:, :]).astype(BF16)
    d_v = total[:, HD:].astype(BF16)
    d_shared[:HD, :] = t_mm(d_k, normed[...]).astype(BF16)
    d_shared[HD:, :] = t_mm(d_v, normed[...]).astype(BF16)
    grad = d_normed[...] + mm_t(d_k, wk[...]) + mm_t(d_v, wv[...])
    to_x, to_gain = norm_back(x_ref[...].astype(F32), gain[...], grad)
    d_x[...] = (d_hidden[...] + to_x).astype(BF16)
    d_gain[...] = to_gain[None]


def input_back(d_kv, behind, normed, d_normed, x, d_hidden, w, place):
    cos, sin = place[:2]
    rows, width = normed.shape
    ops = (
        d_kv, behind, normed, w["key"], w["value"], d_normed, x, w["gain_attn"], d_hidden, cos, sin,
    )
    return pl.pallas_call(
        input_back_kernel,
        out_shape=(
            jax.ShapeDtypeStruct((rows, width), BF16),
            jax.ShapeDtypeStruct((2 * HD, width), BF16),
            jax.ShapeDtypeStruct((1, width), F32),
        ),
        compiler_params=pltpu.CompilerParams(vmem_limit_bytes=56 * 1024 * 1024),
        cost_estimate=SMALL,
    )(*ops)


def pack_shared(d_shared, d_gain_attn, d_gain_ff, order):
    gains = jnp.concatenate([d_gain_attn, d_gain_ff])
    gains = jnp.pad(gains, ((0, GAIN_ROWS - 2), (0, 0))).astype(BF16)
    count = d_shared.shape[0] // STEPS
    pieces = []
    for j in range(STEPS):
        quarter = lax.dynamic_slice_in_dim(d_shared, (order ^ j) * count, count, 0)
        pieces.append(jnp.concatenate([quarter, gains]))
    return jnp.stack(pieces[:2]), jnp.stack(pieces[2:])


def over_cores(near, got):
    return jnp.concatenate([a + b for a, b in zip(near, got)], axis=1)


def finish_part(scale, source, at, size):
    return source[at : at + size, :].astype(F32) * scale


def for_core(core, put, mine, other):
    @pl.when(core[0] == 0)
    def _():
        put(0, *mine)
        put(1, *other)

    @pl.when(core[0] != 0)
    def _():
        put(0, *other)
        put(1, *mine)


def finish_ffn_kernel(scale, core, *refs):
    gate, up, down = refs[4:]
    units = gate.shape[1] // 2
    part = functools.partial(finish_part, scale)

    def put(core, low, high):
        at, step = core * units, units // 4
        gate[:, at : at + 3 * step] = part(low, 0, 3 * step).T
        gate[:, at + 3 * step : at + units] = part(high, 0, step).T
        up[:, at : at + 2 * step] = part(high, step, 2 * step).T
        up[:, at + 2 * step : at + units] = part(low, 3 * step, 2 * step).T
        down[at : at + step, :] = part(low, 5 * step, step)
        down[at + step : at + units, :] = part(high, 3 * step, 3 * step)

    for_core(core, put, refs[:2], refs[2:4])


def finish_attn_kernel(scale, core, *refs):
    shared = refs[4]
    query, key, value, out = refs[5:]
    heads = query.shape[1] // 2
    part = functools.partial(finish_part, scale)

    def put(core, low, high):
        some, at = low.shape[0] - heads, core * heads
        query[:, at : at + heads] = part(low, 0, heads).T
        out[at : at + some, :] = part(low, heads, some)
        out[at + some : at + heads, :] = part(high, 0, heads - some)

    for_core(core, put, refs[:2], refs[2:4])
    key[...] = part(shared, 0, HD).T
    value[...] = part(shared, HD, HD).T


def finish(kernel, shapes, core, scale, *ops):
    vmem = pl.BlockSpec(memory_space=pltpu.VMEM)
    return pl.pallas_call(
        functools.partial(kernel, scale),
        out_shape=[jax.ShapeDtypeStruct(shape, F32) for shape in shapes],
        in_specs=[pl.BlockSpec(memory_space=pltpu.SMEM)] + [vmem] * len(ops),
        out_specs=[vmem] * len(shapes),
        compiler_params=pltpu.CompilerParams(vmem_limit_bytes=56 * 1024 * 1024),
        cost_estimate=SMALL,
    )(core.reshape(1), *ops)


def finish_ffn(mine, other, core, scale, units):
    width = mine[0].shape[1]
    shapes = [(width, units), (width, units), (units, width)]
    return finish(finish_ffn_kernel, shapes, core, scale, *mine, *other)


def finish_attn(mine, other, shared, core, scale, heads):
    width = shared.shape[1]
    shapes = [(width, heads), (width, HD), (width, HD), (heads, width)]
    return finish(finish_attn_kernel, shapes, core, scale, *mine, *other, shared)


def halves(total, section, axis):
    half = total.shape[axis] // 2
    low, high = (lax.slice_in_dim(total, i * half, (i + 1) * half, axis=axis) for i in range(2))
    return pick(section == 0, low, high), pick(section == 0, high, low)


def shifted(value, axis, steps):
    count = lax.axis_size(axis)
    return lax.ppermute(value, axis, [(i, (i + steps) % count) for i in range(count)])


def share(value, axis, steps):
    count = lax.axis_size(axis)
    rows = value.shape[0] // count
    place = lax.rem(lax.axis_index(axis) + steps, count)
    return lax.dynamic_slice_in_dim(value, place * rows, rows, 0)


def local(
    x_input,
    doc_lengths,
    cotangent,
    gain_attn,
    w_query,
    w_key,
    w_value,
    w_out,
    gain_ff,
    w_gate,
    w_up,
    w_down,
):
    section = lax.axis_index("section")
    gx, gy = lax.axis_index("gx"), lax.axis_index("gy")
    own_rows = x_input.shape[2]
    scale = 1.0 / lax.axis_size("dp")

    def mine(value):
        return lax.dynamic_index_in_dim(value[:, 0], section, 0, keepdims=False)

    x = mine(x_input)
    first, x_before, finish_weights = gather_weights(
        x, w_query[0], w_key[0], w_value[0], w_out[0], w_gate[0], w_up[0], w_down[0], section
    )
    gains = jnp.concatenate([gain_attn, gain_ff])
    other_gains = swap(gains, "section")
    gains = [pick(section == layer, gains, other_gains) for layer in range(2)]
    first.update(gain_attn=gains[0][:1], gain_ff=gains[0][1:])

    x_all = jnp.concatenate([x_before, x])
    start = (gx * lax.axis_size("gy") + gy) * own_rows
    rows = start - WINDOW + jnp.arange(WINDOW + own_rows, dtype=jnp.int32)
    segment, where_in, valid = layout(mine(doc_lengths), rows)
    frequency = jnp.exp(jnp.arange(HD // 2, dtype=F32) * (-2.0 * math.log(10000.0) / HD))
    angles = where_in.astype(F32)[:, None] * frequency[None, :]
    place = (jnp.cos(angles), jnp.sin(angles), segment[WINDOW:, None], segment[None, :])

    q_0, mixed_0, kv_0, normed_0, hidden_0 = attn_forward(x_all, first, place)
    hidden_0, second = finish_weights(hidden_0)
    out_0 = ffn_forward(hidden_0, first)
    out_0, rows_before, second = second(out_0)
    second.update(gain_attn=gains[1][:1], gain_ff=gains[1][1:])
    out_all = jnp.concatenate([rows_before, out_0])
    slot = lambda *values: lax.optimization_barrier(values)
    q_1, mixed_1, kv_1, normed_1, hidden_1 = attn_forward(out_all, second, place)
    hidden_1, up_1 = slot(hidden_1, second["up"])
    up_1 = jnp.stack(up_1)
    second.update(up=(up_1, swap(up_1, "gx")))

    def by_micro(own, other):
        first = section == 0
        return jnp.stack([jnp.where(first, own, other), jnp.where(first, other, own)])[
            None, :, None
        ]

    order = 2 * gx + gy
    dy = jnp.where(valid[WINDOW:, None], mine(cotangent), 0)
    turn = 3 * w_gate.shape[2] // 4

    def ffn_parts(near, got):
        a_near, a_far = (near[i, :turn] + got[i, :turn] for i in range(2))
        return a_near, a_far, near[:, turn:] + got[:, turn:]

    far, before = ffn_back(dy, hidden_1, second, 1)
    before, far = slot(before, far)
    got = swap(far, "gx")
    near, d_hidden, gain_ff = ffn_back(dy, hidden_1, second, 0, before)
    near, d_hidden, gain_ff, got = slot(near, d_hidden, gain_ff, got)
    a_near, a_far, b = ffn_parts(near, got)
    b_keep, b_send = halves(b, section, 1)
    a_got = swap(a_far, "gy")
    b_got = swap(b_send, "section")
    out_1 = ffn_forward(hidden_1, second)
    out_near, out_far, d_q, sent, d_kv = attn_back(
        d_hidden, q_1, mixed_1, kv_1, second, place
    )
    d_q, sent, out_1, a_got, b_got = slot(d_q, sent, out_1, a_got, b_got)
    a_keep, a_send = halves(a_near + a_got, section, 0)
    b = b_keep + b_got
    behind = to_before(sent)
    a_got = swap(a_send, "section")
    query_near, query_far, d_normed = query_back(d_q, normed_1, second)
    query_got, out_got = swap(query_far, "gx"), swap(out_far, "gx")
    d_normed, behind, b, a_got = slot(d_normed, behind, b, a_got)
    b_far = swap(b[1], "gy")
    grad_1, d_shared, gain_attn_grad = input_back(
        d_kv, behind, normed_1, d_normed, out_0, d_hidden, second, place
    )
    near, far = pack_shared(d_shared, gain_attn_grad, gain_ff, order)
    near, got = (query_near, out_near, near), (query_got, out_got, swap(far, "gx"))
    grad_1, near, got = slot(grad_1, near, got)

    c_keep_1, c_send_1 = halves(over_cores(near, got), section, 1)
    c_send_a, c_send_b = c_send_1[0], c_send_1[1]
    c_got_a = swap(c_send_a, "section")
    far, before = ffn_back(grad_1, hidden_0, first, 1)
    before, far, b_far, c_got_a = slot(before, far, b_far, c_got_a)
    ffn_1 = jnp.concatenate([a_keep + a_got, b[0] + b_far])
    direct = lax.axis_size("dp") == 4
    terms = [share(ffn_1, "dp", steps) for steps in range(4)] if direct else []
    some = [shifted(terms[steps], "dp", steps) for steps in (1, 3)] if direct else []
    got = swap(far, "gx")
    c_got_b = swap(c_send_b, "section")
    near, d_hidden, gain_ff = ffn_back(grad_1, hidden_0, first, 0, before)
    near, d_hidden, gain_ff, got, c_got_b, some, terms = slot(
        near, d_hidden, gain_ff, got, c_got_b, some, terms
    )
    some += [shifted(terms[2], "dp", 2)] if direct else []
    a_near, a_far, b = ffn_parts(near, got)
    b_keep, b_send = halves(b, section, 1)
    b_got = swap(b_send, "section")
    a_got = swap(a_far, "gy")
    out_near, out_far, d_q, sent, d_kv = attn_back(
        d_hidden, q_0, mixed_0, kv_0, first, place
    )
    c_1 = [c_keep_1[0] + c_got_a, c_keep_1[1] + c_got_b]
    d_q, sent, some = slot(d_q, sent, some)
    if direct:
        mine_1 = sum((value.astype(F32) for value in some), terms[0].astype(F32)).astype(BF16)
        some = [mine_1, shifted(mine_1, "dp", 1)]
    behind = to_before(sent)
    query_near, query_far, d_normed = query_back(d_q, normed_0, first)
    query_got, out_got = swap(query_far, "gx"), swap(out_far, "gx")
    d_normed, behind, b_got, a_got, some = slot(d_normed, behind, b_got, a_got, some)
    b = b_keep + b_got
    b_far = swap(b[1], "gy")
    a_keep, a_send = halves(a_near + a_got, section, 0)
    a_got = swap(a_send, "section")
    some += [shifted(some[0], "dp", steps) for steps in (2, 3)] if direct else []
    grad_0, d_shared, gain_attn_grad = input_back(
        d_kv, behind, normed_0, d_normed, x, d_hidden, first, place
    )
    grad_0, d_shared, a_got, b_far, some = slot(grad_0, d_shared, a_got, b_far, some)
    ffn_0 = jnp.concatenate([a_keep + a_got, b[0] + b_far])
    if direct:
        ffn_0 = lax.psum(ffn_0, "dp")
        found = jnp.stack(some)
        place = lax.axis_index("dp")
        ffn_1 = jnp.concatenate(
            [
                lax.dynamic_index_in_dim(found, lax.rem(place + 4 - i, 4), 0, keepdims=False)
                for i in range(4)
            ]
        )
    else:
        ffn_1, ffn_0 = lax.psum((ffn_1, ffn_0), "dp")
    near, far = pack_shared(d_shared, gain_attn_grad, gain_ff, order)
    near, got = (query_near, out_near, near), (query_got, out_got, swap(far, "gx"))
    c_keep, c_send = halves(over_cores(near, got), section, 1)
    c_got = swap(c_send, "section")
    c_far_1 = swap(c_1[1], "gy")
    c_keep, c_got, c_far_1, grad_0 = slot(c_keep, c_got, c_far_1, grad_0)
    c = c_keep + c_got
    c_far = swap(c[1], "gy")
    first_rows, second_rows = (jnp.concatenate(rows) for rows in ((out_0, grad_0), (out_1, grad_1)))
    others = swap(pick(section == 0, second_rows, first_rows), "section")
    ffn_0, ffn_1, c_far = slot(ffn_0, ffn_1, c_far)
    attn = jnp.concatenate([c_1[0] + c_far_1, c[0] + c_far])
    sent = pick(section == 0, ffn_1, ffn_0)
    ffn_got = swap(sent, "section")
    attn = lax.psum(attn, "dp")
    attn, ffn_got, others = slot(attn, ffn_got, others)

    def two_halves(one, zero, got):
        mine = pick(section == 0, zero, one)
        return pick(section == 0, mine, got), pick(section == 0, got, mine)

    half = attn.shape[0] // 2
    attn_got = swap(pick(section == 0, attn[:half], attn[half:]), "section")
    ffn_mine = two_halves(ffn_1, ffn_0, ffn_got)
    gate, up, down = finish_ffn(
        ffn_mine, [swap(value, "gx") for value in ffn_mine], gx, scale, w_gate.shape[2]
    )
    states = by_micro(pick(section == 0, out_0, out_1), others[:own_rows])
    in_grads = by_micro(pick(section == 0, grad_0, grad_1), others[own_rows:])
    attn_got, gate, up, down, states, in_grads = slot(attn_got, gate, up, down, states, in_grads)
    attn_low, high = two_halves(attn[:half], attn[half:], attn_got)
    attn_others = swap(attn_low, "gx"), swap(high, "gx")
    count = d_shared.shape[0] // STEPS
    quarter = high[-GAIN_ROWS - count : -GAIN_ROWS]
    gain_sums = high[-GAIN_ROWS : 2 - GAIN_ROWS].astype(F32) * scale
    beside = swap(quarter, "gy")
    both = pick(
        gy == 0, jnp.concatenate([quarter, beside]), jnp.concatenate([beside, quarter])
    )
    both_other = swap(both, "gx")
    shared = pick(
        gx == 0, jnp.concatenate([both, both_other]), jnp.concatenate([both_other, both])
    )
    query, key, value, out = finish_attn(
        (attn_low, high), attn_others, shared, gx, scale, w_query.shape[2]
    )

    return (
        states,
        in_grads,
        gain_sums[:1],
        query[None],
        key[None],
        value[None],
        out[None],
        gain_sums[1:],
        gate[None],
        up[None],
        down[None],
    )


def solution(mesh):
    rows = P(None, "dp", ("gx", "gy"), None)
    columns = P("section", None, "gy")
    depth = P("section", "gy", None)
    whole = P("section", None, None)
    gain = P("section", None)
    by_layer = P("section", None, "dp", ("gx", "gy"), None)
    return jax.shard_map(
        local,
        mesh=mesh,
        in_specs=(
            rows,
            P(None, "dp", None),
            rows,
            gain,
            columns,
            whole,
            whole,
            depth,
            gain,
            columns,
            columns,
            depth,
        ),
        out_specs=(
            by_layer,
            by_layer,
            gain,
            columns,
            whole,
            whole,
            depth,
            gain,
            columns,
            columns,
            depth,
        ),
        check_vma=False,
    )
```

```python
import functools
import math

import jax
import jax.numpy as jnp
from jax import lax
from jax.experimental import pallas as pl
from jax.experimental.pallas import tpu as pltpu
from jax.sharding import PartitionSpec as P

HD = 256
WINDOW = 512
GAIN_ROWS = 32
F32 = jnp.float32
BF16 = jnp.bfloat16


def swap(value, axis):
    return lax.ppermute(value, axis, [(0, 1), (1, 0)])


def mm(a, b):
    return jnp.dot(a, b, preferred_element_type=F32)


def mm_t(a, b):
    return lax.dot_general(a, b, (((1,), (1,)), ((), ())), preferred_element_type=F32)


def t_mm(a, b):
    return lax.dot_general(a, b, (((0,), (0,)), ((), ())), preferred_element_type=F32)


def inverse_rms(value):
    return lax.rsqrt(jnp.mean(value * value, axis=-1, keepdims=True) + 1e-06)


def norm_back(value, gain, grad):
    s = inverse_rms(value)
    scaled = grad * gain
    to_value = s * scaled - value * (s * s * s) * jnp.mean(value * scaled, axis=-1, keepdims=True)
    return to_value, jnp.sum(grad * value * s, axis=0)


def rotate(value, cos, sin):
    half = value.shape[-1] // 2
    a, b = value[..., :half], value[..., half:]
    return jnp.concatenate([a * cos - b * sin, b * cos + a * sin], axis=-1)


def unrotate(value, cos, sin):
    half = value.shape[-1] // 2
    c, e = value[..., :half], value[..., half:]
    return jnp.concatenate([c * cos + e * sin, e * cos - c * sin], axis=-1)


def gelu_parts(v):
    c = math.sqrt(2.0 / math.pi)
    t = jnp.tanh(c * (v + 0.044715 * v * v * v))
    value = 0.5 * v * (1.0 + t)
    slope = 0.5 * (1.0 + t) + 0.5 * v * (1.0 - t * t) * (c * (1.0 + 3 * 0.044715 * v * v))
    return value, slope


def layout(lengths, rows):
    docs = lengths.shape[0]
    ends = jnp.cumsum(lengths)
    number = jnp.sum((rows[:, None] >= ends[None, :]).astype(jnp.int32), axis=1)
    valid = number < docs
    begin = jnp.sum(
        jnp.where(number[:, None] == jnp.arange(docs)[None, :], (ends - lengths)[None, :], 0), axis=1
    )
    place = jnp.where(valid, rows - begin, 0)
    segment = jnp.where(rows < 0, -1, jnp.where(valid, number, docs + rows))
    return segment, place, valid


def pick(flag, a, b):
    return jnp.where(flag, a, b)


def gather_weights(x, w_query, w_key, w_value, w_out, w_gate, w_up, w_down, section):
    gx = lax.axis_index("gx")
    barrier = lax.optimization_barrier

    def half(w, axis):
        size = w.shape[axis] // 2
        return lax.dynamic_slice_in_dim(w, gx * size, size, axis)

    def two_layers(mine, received):
        return [pick(section == layer, mine, received) for layer in range(2)]

    def over_gx(own, beside):
        both = jnp.stack([own, beside])
        return both, swap(both, "gx")

    heads = w_query.shape[1] // 2
    first_own = jnp.concatenate([half(w_query, 1), half(w_key, 1), half(w_value, 1)], axis=1)
    out_own, gate_own, up_own, down_own = half(w_out, 0), half(w_gate, 1), half(w_up, 1), half(w_down, 0)
    first_got = swap(first_own, "section")
    x_before = from_before(x)
    out_got = swap(out_own, "section")
    down_beside = swap(down_own, "gy")
    first_got, gate_own = barrier((first_got, gate_own))

    queries = two_layers(first_own[:, :heads], first_got[:, :heads])
    query_beside = swap(queries[0], "gy")
    gate_got = swap(gate_own, "section")
    shared_got = first_got[:, heads:]
    shared_other = swap(shared_got, "gx")
    out_got, up_own = barrier((out_got, up_own))

    outs = two_layers(out_own, out_got)
    out_beside = swap(outs[0], "gy")
    up_got = swap(up_own, "section")
    low, high = pick(gx == 0, shared_got, shared_other), pick(gx == 0, shared_other, shared_got)
    part = low.shape[1] // 2
    key_got = jnp.concatenate([low[:, :part], high[:, :part]], axis=1)
    value_got = jnp.concatenate([low[:, part:], high[:, part:]], axis=1)
    keys, values = two_layers(w_key, key_got), two_layers(w_value, value_got)
    down_pair = jnp.stack([down_own, down_beside])
    gate_got, down_pair, keys, values = barrier((gate_got, down_pair, keys, values))

    gates = two_layers(gate_own, gate_got)
    gate_beside = swap(gates[0], "gy")
    down_got = swap(down_pair, "section")
    query_beside, out_beside, x_before, up_got = barrier((query_beside, out_beside, x_before, up_got))
    ups = two_layers(up_own, up_got)
    up_beside = swap(ups[0], "gy")
    later = queries[1], outs[1]
    later_besides = [swap(value, "gy") for value in later]
    first = {
        "query": over_gx(queries[0], query_beside),
        "out": over_gx(outs[0], out_beside),
        "key": keys[0],
        "value": values[0],
    }

    def finish(kernel_out):
        kernel_out, gate_here, up_here, arrived, gate_1 = barrier(
            (kernel_out, gate_beside, up_beside, later_besides, gates[1])
        )
        gate_1_beside = swap(gate_1, "gy")
        downs = two_layers(down_pair, down_got)
        first.update(
            gate=over_gx(gates[0], gate_here),
            up=over_gx(ups[0], up_here),
            down=(downs[0], swap(downs[0], "gx")),
        )

        def second(kernel_out):
            kernel_out, gate_1_here, up_1, down_1 = barrier(
                (kernel_out, gate_1_beside, ups[1], downs[1])
            )
            rows_before = from_before(kernel_out)
            down_pairs = down_1, swap(down_1, "gx")
            query_pairs, out_pairs = over_gx(later[0], arrived[0]), over_gx(later[1], arrived[1])
            gate_pairs = over_gx(gate_1, gate_1_here)
            rows_before, up_1, gate_pairs, down_pairs, query_pairs, out_pairs = barrier(
                (rows_before, up_1, gate_pairs, down_pairs, query_pairs, out_pairs)
            )
            layer = {
                "query": query_pairs,
                "out": out_pairs,
                "gate": gate_pairs,
                "up": (up_1, swap(up_1, "gy")),
                "down": down_pairs,
                "key": keys[1],
                "value": values[1],
            }
            return kernel_out, rows_before, layer

        return kernel_out, second

    return first, x_before, finish


def from_before(value):
    return lax.ppermute(value, ("gx", "gy"), [(0, 1), (1, 2), (2, 3)])


def to_before(value):
    return lax.ppermute(value, ("gx", "gy"), [(1, 0), (2, 1), (3, 2)])


BLOCK = 256
STEPS = 4
PARAMS = dict(
    grid=(STEPS,),
    compiler_params=pltpu.CompilerParams(
        dimension_semantics=("arbitrary",), vmem_limit_bytes=56 * 1024 * 1024
    ),
)


def all_of(shape):
    return pl.BlockSpec(shape, lambda j: (0,) * len(shape))


def step_of(shape):
    return pl.BlockSpec((1,) + shape[1:], lambda j: (j,) + (0,) * (len(shape) - 1))


def first_of(shape):
    return pl.BlockSpec((1,) + shape[1:], lambda j: (jnp.minimum(j, 1),) + (0,) * (len(shape) - 1))


def last_of(shape):
    return pl.BlockSpec(
        (1,) + shape[1:], lambda j: (jnp.maximum(j - 2, 0),) + (0,) * (len(shape) - 1)
    )


SMALL = pl.CostEstimate(flops=1000, bytes_accessed=1000, transcendentals=0)


def take(step, first, last, held):
    @pl.when(step < 2)
    def _():
        held[...] = first[0]

    @pl.when(step >= 2)
    def _():
        held[...] = last[0]


def bias_of(seg_q, seg_k, first, rows, keys, before):
    distance = (
        lax.broadcasted_iota(jnp.int32, (rows, keys), 0)
        + before
        - lax.broadcasted_iota(jnp.int32, (rows, keys), 1)
    )
    same = seg_q[first : first + rows, :] == seg_k[:, first : first + keys]
    return jnp.where((distance >= 0) & (distance < WINDOW) & same, 0.0, -1e30)


def softmax(scores):
    weights = jnp.exp(scores - jnp.max(scores, axis=-1, keepdims=True))
    return weights * (1.0 / jnp.sum(weights, axis=-1, keepdims=True))


def attn_kernel(
    x_ref, gain, wq_a, wq_b, wk, wv, wo_a, wo_b, cos, sin, seg_q, seg_k,
    q_out, mixed_out, kv_out, normed_out, hidden_out,
):
    rows = normed_out.shape[0]
    before = x_ref.shape[0] - rows
    x = x_ref[...].astype(F32)
    normed = (x * inverse_rms(x) * gain[...]).astype(BF16)
    normed_out[...] = normed[before:]
    kv_out[:, :HD] = rotate(mm(normed, wk[...]), cos[...], sin[...]).astype(BF16)
    kv_out[:, HD:] = mm(normed, wv[...]).astype(BF16)
    for j in range(STEPS):
        wq = (wq_a, wq_b)[j // 2][j % 2]
        q = rotate(mm(normed_out[...], wq), cos[before:, :], sin[before:, :]) * HD**-0.5
        q_out[j] = q.astype(BF16)
    for at in range(0, rows, BLOCK):
        here = pl.ds(at, BLOCK)
        count = before + BLOCK
        keys = pl.ds(at, count)
        bias = bias_of(seg_q, seg_k, at, BLOCK, count, before)
        q = q_out[:, here, :].reshape(STEPS * BLOCK, HD)
        scores = mm_t(q, kv_out[keys, :HD]).reshape(STEPS, BLOCK, count) + bias[None]
        probs = softmax(scores).astype(BF16).reshape(STEPS * BLOCK, count)
        mixed = mm(probs, kv_out[keys, HD:]).astype(BF16).reshape(STEPS, BLOCK, HD)
        mixed_out[:, here, :] = mixed
        hidden = x_ref[pl.ds(before + at, BLOCK), :].astype(F32)
        for j in range(STEPS):
            hidden = hidden + mm(mixed[j], (wo_a, wo_b)[j // 2][j % 2])
        hidden_out[here, :] = hidden


WHOLE = dict(
    compiler_params=pltpu.CompilerParams(vmem_limit_bytes=56 * 1024 * 1024), cost_estimate=SMALL
)


def attn_forward(x_all, w, place):
    cos, sin, seg_q, seg_k = place
    total, width = x_all.shape
    rows = seg_q.shape[0]
    heads = (STEPS, rows, HD)
    ops = (x_all, w["gain_attn"], *w["query"], w["key"], w["value"], *w["out"], cos, sin, seg_q, seg_k)
    return pl.pallas_call(
        attn_kernel,
        out_shape=(
            jax.ShapeDtypeStruct(heads, BF16),
            jax.ShapeDtypeStruct(heads, BF16),
            jax.ShapeDtypeStruct((total, 2 * HD), BF16),
            jax.ShapeDtypeStruct((rows, width), BF16),
            jax.ShapeDtypeStruct((rows, width), F32),
        ),
        **WHOLE,
    )(*ops)


def ffn_kernel(
    hidden, gain, gate_a, gate_b, up_a, up_b, down_a, down_b,
    out, normed, total, w_gate, w_up, down,
):
    j = pl.program_id(0)

    @pl.when(j == 0)
    def _():
        value = hidden[...]
        normed[...] = (value * inverse_rms(value) * gain[...]).astype(BF16)
        total[...] = value

    take(j, gate_a, gate_b, w_gate)
    take(j, up_a, up_b, w_up)
    take(j, down_a, down_b, down)
    gate = mm(normed[...], w_gate[...])
    up = mm(normed[...], w_up[...])
    act = (gelu_parts(gate)[0] * up).astype(BF16)
    total[...] += mm(act, down[...])

    @pl.when(j == STEPS - 1)
    def _():
        out[...] = total[...].astype(BF16)


def ffn_forward(hidden, w):
    rows, width = hidden.shape
    ops = (hidden, w["gain_ff"], *w["gate"], *w["up"], *w["down"])
    units = w["down"][0].shape[1]
    pairs = {i: (first_of, last_of)[i % 2] for i in range(2, 8)}
    return pl.pallas_call(
        ffn_kernel,
        out_shape=jax.ShapeDtypeStruct((rows, width), BF16),
        in_specs=[pairs.get(i, all_of)(op.shape) for i, op in enumerate(ops)],
        out_specs=all_of((rows, width)),
        scratch_shapes=[
            pltpu.VMEM((rows, width), BF16),
            pltpu.VMEM((rows, width), F32),
            pltpu.VMEM((width, units), BF16),
            pltpu.VMEM((width, units), BF16),
            pltpu.VMEM((units, width), BF16),
        ],
        cost_estimate=SMALL,
        **PARAMS,
    )(*ops)


def ffn_back_kernel(last, dy, hidden, gain, before, gate, up, down, out, *rest):
    total, normed = rest[-2:]
    j = pl.program_id(0)
    units = down.shape[1]

    @pl.when(j == 0)
    def _():
        value = hidden[...]
        normed[...] = (value * inverse_rms(value) * gain[...]).astype(BF16)
        total[...] = before[...] if last else jnp.zeros_like(total)

    gate_value = mm(normed[...], gate[0])
    up_value = mm(normed[...], up[0])
    d_act = mm_t(dy[...], down[0])
    value, slope = gelu_parts(gate_value)
    act = (value * up_value).astype(BF16)
    d_gate = (d_act * up_value * slope).astype(BF16)
    d_up = (d_act * value).astype(BF16)
    total[...] += mm_t(d_gate, gate[0]) + mm_t(d_up, up[0])
    for i, part in enumerate((t_mm(d_gate, normed[...]), t_mm(d_up, normed[...]), t_mm(act, dy[...]))):
        out[0, pl.ds(i * units, units), :] = part.astype(BF16)

    @pl.when(j == pl.num_programs(0) - 1)
    def _():
        if last:
            d_hidden, d_gain = rest[:2]
            to_hidden, to_gain = norm_back(hidden[...], gain[...], total[...])
            d_hidden[...] = dy[...].astype(F32) + to_hidden
            d_gain[...] = to_gain[None]
        else:
            rest[0][...] = total[...]


def ffn_back(dy, hidden, w, pair, before=None):
    rows, width = hidden.shape
    last = before is not None
    ops = (dy, hidden, w["gain_ff"], before if last else jnp.zeros((8, 128), F32))
    ops += (w["gate"][pair], w["up"][pair], w["down"][pair])
    packed = (2, 3 * w["down"][pair].shape[1], width)
    shapes = [(rows, width), (1, width)] if last else [(rows, width)]
    return pl.pallas_call(
        functools.partial(ffn_back_kernel, last),
        grid=(2,),
        out_shape=[jax.ShapeDtypeStruct(packed, BF16)]
        + [jax.ShapeDtypeStruct(shape, F32) for shape in shapes],
        in_specs=[all_of(op.shape) for op in ops[:4]] + [step_of(op.shape) for op in ops[4:]],
        out_specs=[step_of(packed)] + [all_of(shape) for shape in shapes],
        scratch_shapes=[pltpu.VMEM((rows, width), F32), pltpu.VMEM((rows, width), BF16)],
        compiler_params=pltpu.CompilerParams(
            dimension_semantics=("arbitrary",), vmem_limit_bytes=56 * 1024 * 1024
        ),
        cost_estimate=SMALL,
    )(*ops)


def put_pair(step, near, far, value):
    @pl.when(step < 2)
    def _():
        near[0] = value

    @pl.when(step >= 2)
    def _():
        far[0] = value


def attn_back_kernel(
    d_hidden, q_ref, mixed, kv, wo_a, wo_b, cos, sin, seg_q, seg_k,
    near, far, d_q, sent, own, d_kv,
):
    rows = d_hidden.shape[0]
    before = kv.shape[0] - rows
    grad = d_hidden[...].astype(BF16)
    for j in range(STEPS):
        (near, far)[j // 2][j % 2, :, :] = t_mm(mixed[j], grad).astype(BF16)
    for at in range(0, rows, BLOCK):
        here = pl.ds(at, BLOCK)
        place = pl.ds(before + at, BLOCK)
        count = before + BLOCK
        keys = pl.ds(at, count)
        bias = bias_of(seg_q, seg_k, at, BLOCK, count, before)
        q = q_ref[:, here, :].reshape(STEPS * BLOCK, HD)
        g = grad[at : at + BLOCK]
        d_mixed = jnp.concatenate(
            [mm_t(g, (wo_a, wo_b)[j // 2][j % 2]).astype(BF16) for j in range(STEPS)]
        )
        probs = softmax(mm_t(q, kv[keys, :HD]).reshape(STEPS, BLOCK, count) + bias[None])
        d_probs = mm_t(d_mixed, kv[keys, HD:]).reshape(STEPS, BLOCK, count)
        inner = jnp.sum(probs * d_probs, axis=-1, keepdims=True)
        d_scores = (probs * (d_probs - inner)).astype(BF16).reshape(STEPS * BLOCK, count)
        low = probs.astype(BF16).reshape(STEPS * BLOCK, count)
        back = mm(d_scores, kv[keys, :HD]).reshape(STEPS, BLOCK, HD)
        back = unrotate(back, cos[place, :][None], sin[place, :][None]) * HD**-0.5
        d_q[:, here, :] = back.astype(BF16)
        d_k, d_v = t_mm(d_scores, q), t_mm(low, d_mixed)
        if at == 0:
            d_kv[keys, :HD], d_kv[keys, HD:] = d_k, d_v
        else:
            done = pl.ds(at, count - BLOCK)
            last = pl.ds(at + count - BLOCK, BLOCK)
            d_kv[done, :HD] += d_k[: count - BLOCK]
            d_kv[done, HD:] += d_v[: count - BLOCK]
            d_kv[last, :HD], d_kv[last, HD:] = d_k[count - BLOCK :], d_v[count - BLOCK :]
    sent[...] = d_kv[:before, :].astype(BF16)
    own[...] = d_kv[before:, :]


def attn_back(d_hidden, q, mixed, kv, w, place):
    rows, width = d_hidden.shape
    total = kv.shape[0]
    ops = (d_hidden, q, mixed, kv, *w["out"], *place)
    return pl.pallas_call(
        attn_back_kernel,
        out_shape=(
            jax.ShapeDtypeStruct((2, HD, width), BF16),
            jax.ShapeDtypeStruct((2, HD, width), BF16),
            jax.ShapeDtypeStruct(q.shape, BF16),
            jax.ShapeDtypeStruct((total - rows, 2 * HD), BF16),
            jax.ShapeDtypeStruct((rows, 2 * HD), F32),
        ),
        scratch_shapes=[pltpu.VMEM((total, 2 * HD), F32)],
        **WHOLE,
    )(*ops)


def query_back_kernel(d_q, normed, wq_a, wq_b, near, far, d_normed):
    total = None
    for j in range(STEPS):
        (near, far)[j // 2][j % 2, :, :] = t_mm(d_q[j], normed[...]).astype(BF16)
        term = mm_t(d_q[j], (wq_a, wq_b)[j // 2][j % 2])
        total = term if total is None else total + term
    d_normed[...] = total


def query_back(d_q, normed, w):
    rows, width = normed.shape
    return pl.pallas_call(
        query_back_kernel,
        out_shape=(
            jax.ShapeDtypeStruct((2, HD, width), BF16),
            jax.ShapeDtypeStruct((2, HD, width), BF16),
            jax.ShapeDtypeStruct((rows, width), F32),
        ),
        **WHOLE,
    )(d_q, normed, *w["query"])


def input_back_kernel(
    d_kv, behind, normed, wk, wv, d_normed, x_ref, gain, d_hidden, cos, sin, d_x, d_shared, d_gain
):
    before = cos.shape[0] - normed.shape[0]
    total = d_kv[...] + behind[...].astype(F32)
    d_k = unrotate(total[:, :HD], cos[before:, :], sin[before:, :]).astype(BF16)
    d_v = total[:, HD:].astype(BF16)
    d_shared[:HD, :] = t_mm(d_k, normed[...]).astype(BF16)
    d_shared[HD:, :] = t_mm(d_v, normed[...]).astype(BF16)
    grad = d_normed[...] + mm_t(d_k, wk[...]) + mm_t(d_v, wv[...])
    to_x, to_gain = norm_back(x_ref[...].astype(F32), gain[...], grad)
    d_x[...] = (d_hidden[...] + to_x).astype(BF16)
    d_gain[...] = to_gain[None]


def input_back(d_kv, behind, normed, d_normed, x, d_hidden, w, place):
    cos, sin = place[:2]
    rows, width = normed.shape
    ops = (
        d_kv, behind, normed, w["key"], w["value"], d_normed, x, w["gain_attn"], d_hidden, cos, sin,
    )
    return pl.pallas_call(
        input_back_kernel,
        out_shape=(
            jax.ShapeDtypeStruct((rows, width), BF16),
            jax.ShapeDtypeStruct((2 * HD, width), BF16),
            jax.ShapeDtypeStruct((1, width), F32),
        ),
        compiler_params=pltpu.CompilerParams(vmem_limit_bytes=56 * 1024 * 1024),
        cost_estimate=SMALL,
    )(*ops)


def pack_shared(d_shared, d_gain_attn, d_gain_ff, order):
    gains = jnp.concatenate([d_gain_attn, d_gain_ff])
    gains = jnp.pad(gains, ((0, GAIN_ROWS - 2), (0, 0))).astype(BF16)
    count = d_shared.shape[0] // STEPS
    pieces = []
    for j in range(STEPS):
        quarter = lax.dynamic_slice_in_dim(d_shared, (order ^ j) * count, count, 0)
        pieces.append(jnp.concatenate([quarter, gains]))
    return jnp.stack(pieces[:2]), jnp.stack(pieces[2:])


def over_cores(near, got):
    return jnp.concatenate([a + b for a, b in zip(near, got)], axis=1)


def finish_part(scale, source, at, size):
    return source[at : at + size, :].astype(F32) * scale


def for_core(core, put, mine, other):
    @pl.when(core[0] == 0)
    def _():
        put(0, *mine)
        put(1, *other)

    @pl.when(core[0] != 0)
    def _():
        put(0, *other)
        put(1, *mine)


def finish_ffn_kernel(scale, core, *refs):
    gate, up, down = refs[4:]
    units = gate.shape[1] // 2
    part = functools.partial(finish_part, scale)

    def put(core, low, high):
        at, step = core * units, units // 4
        gate[:, at : at + 3 * step] = part(low, 0, 3 * step).T
        gate[:, at + 3 * step : at + units] = part(high, 0, step).T
        up[:, at : at + 2 * step] = part(high, step, 2 * step).T
        up[:, at + 2 * step : at + units] = part(low, 3 * step, 2 * step).T
        down[at : at + step, :] = part(low, 5 * step, step)
        down[at + step : at + units, :] = part(high, 3 * step, 3 * step)

    for_core(core, put, refs[:2], refs[2:4])


def finish_attn_kernel(scale, core, *refs):
    shared = refs[4]
    query, key, value, out = refs[5:]
    heads = query.shape[1] // 2
    part = functools.partial(finish_part, scale)

    def put(core, low, high):
        some, at = low.shape[0] - heads, core * heads
        query[:, at : at + heads] = part(low, 0, heads).T
        out[at : at + some, :] = part(low, heads, some)
        out[at + some : at + heads, :] = part(high, 0, heads - some)

    for_core(core, put, refs[:2], refs[2:4])
    key[...] = part(shared, 0, HD).T
    value[...] = part(shared, HD, HD).T


def finish(kernel, shapes, core, scale, *ops):
    vmem = pl.BlockSpec(memory_space=pltpu.VMEM)
    return pl.pallas_call(
        functools.partial(kernel, scale),
        out_shape=[jax.ShapeDtypeStruct(shape, F32) for shape in shapes],
        in_specs=[pl.BlockSpec(memory_space=pltpu.SMEM)] + [vmem] * len(ops),
        out_specs=[vmem] * len(shapes),
        compiler_params=pltpu.CompilerParams(vmem_limit_bytes=56 * 1024 * 1024),
        cost_estimate=SMALL,
    )(core.reshape(1), *ops)


def finish_ffn(mine, other, core, scale, units):
    width = mine[0].shape[1]
    shapes = [(width, units), (width, units), (units, width)]
    return finish(finish_ffn_kernel, shapes, core, scale, *mine, *other)


def finish_attn(mine, other, shared, core, scale, heads):
    width = shared.shape[1]
    shapes = [(width, heads), (width, HD), (width, HD), (heads, width)]
    return finish(finish_attn_kernel, shapes, core, scale, *mine, *other, shared)


def halves(total, section, axis):
    half = total.shape[axis] // 2
    low, high = (lax.slice_in_dim(total, i * half, (i + 1) * half, axis=axis) for i in range(2))
    return pick(section == 0, low, high), pick(section == 0, high, low)


def shifted(value, axis, steps):
    count = lax.axis_size(axis)
    return lax.ppermute(value, axis, [(i, (i + steps) % count) for i in range(count)])


def share(value, axis, steps):
    count = lax.axis_size(axis)
    rows = value.shape[0] // count
    place = lax.rem(lax.axis_index(axis) + steps, count)
    return lax.dynamic_slice_in_dim(value, place * rows, rows, 0)


def local(
    x_input,
    doc_lengths,
    cotangent,
    gain_attn,
    w_query,
    w_key,
    w_value,
    w_out,
    gain_ff,
    w_gate,
    w_up,
    w_down,
):
    section = lax.axis_index("section")
    gx, gy = lax.axis_index("gx"), lax.axis_index("gy")
    own_rows = x_input.shape[2]
    scale = 1.0 / lax.axis_size("dp")

    def mine(value):
        return lax.dynamic_index_in_dim(value[:, 0], section, 0, keepdims=False)

    x = mine(x_input)
    first, x_before, finish_weights = gather_weights(
        x, w_query[0], w_key[0], w_value[0], w_out[0], w_gate[0], w_up[0], w_down[0], section
    )
    gains = jnp.concatenate([gain_attn, gain_ff])
    other_gains = swap(gains, "section")
    gains = [pick(section == layer, gains, other_gains) for layer in range(2)]
    first.update(gain_attn=gains[0][:1], gain_ff=gains[0][1:])

    x_all = jnp.concatenate([x_before, x])
    start = (gx * lax.axis_size("gy") + gy) * own_rows
    rows = start - WINDOW + jnp.arange(WINDOW + own_rows, dtype=jnp.int32)
    segment, where_in, valid = layout(mine(doc_lengths), rows)
    frequency = jnp.exp(jnp.arange(HD // 2, dtype=F32) * (-2.0 * math.log(10000.0) / HD))
    angles = where_in.astype(F32)[:, None] * frequency[None, :]
    place = (jnp.cos(angles), jnp.sin(angles), segment[WINDOW:, None], segment[None, :])

    q_0, mixed_0, kv_0, normed_0, hidden_0 = attn_forward(x_all, first, place)
    hidden_0, second = finish_weights(hidden_0)
    out_0 = ffn_forward(hidden_0, first)
    out_0, rows_before, second = second(out_0)
    second.update(gain_attn=gains[1][:1], gain_ff=gains[1][1:])
    out_all = jnp.concatenate([rows_before, out_0])
    slot = lambda *values: lax.optimization_barrier(values)
    q_1, mixed_1, kv_1, normed_1, hidden_1 = attn_forward(out_all, second, place)
    hidden_1, up_1 = slot(hidden_1, second["up"])
    up_1 = jnp.stack(up_1)
    second.update(up=(up_1, swap(up_1, "gx")))

    def by_micro(own, other):
        first = section == 0
        return jnp.stack([jnp.where(first, own, other), jnp.where(first, other, own)])[
            None, :, None
        ]

    order = 2 * gx + gy
    dy = jnp.where(valid[WINDOW:, None], mine(cotangent), 0)
    turn = 3 * w_gate.shape[2] // 4

    def ffn_parts(near, got):
        a_near, a_far = (near[i, :turn] + got[i, :turn] for i in range(2))
        return a_near, a_far, near[:, turn:] + got[:, turn:]

    far, before = ffn_back(dy, hidden_1, second, 1)
    before, far = slot(before, far)
    got = swap(far, "gx")
    near, d_hidden, gain_ff = ffn_back(dy, hidden_1, second, 0, before)
    near, d_hidden, gain_ff, got = slot(near, d_hidden, gain_ff, got)
    a_near, a_far, b = ffn_parts(near, got)
    b_keep, b_send = halves(b, section, 1)
    a_got = swap(a_far, "gy")
    b_got = swap(b_send, "section")
    out_1 = ffn_forward(hidden_1, second)
    out_near, out_far, d_q, sent, d_kv = attn_back(
        d_hidden, q_1, mixed_1, kv_1, second, place
    )
    d_q, sent, out_1, a_got, b_got = slot(d_q, sent, out_1, a_got, b_got)
    a_keep, a_send = halves(a_near + a_got, section, 0)
    b = b_keep + b_got
    behind = to_before(sent)
    a_got = swap(a_send, "section")
    query_near, query_far, d_normed = query_back(d_q, normed_1, second)
    query_got, out_got = swap(query_far, "gx"), swap(out_far, "gx")
    d_normed, behind, b, a_got = slot(d_normed, behind, b, a_got)
    b_far = swap(b[1], "gy")
    grad_1, d_shared, gain_attn_grad = input_back(
        d_kv, behind, normed_1, d_normed, out_0, d_hidden, second, place
    )
    near, far = pack_shared(d_shared, gain_attn_grad, gain_ff, order)
    near, got = (query_near, out_near, near), (query_got, out_got, swap(far, "gx"))
    grad_1, near, got = slot(grad_1, near, got)

    c_keep_1, c_send_1 = halves(over_cores(near, got), section, 1)
    c_send_a, c_send_b = c_send_1[0], c_send_1[1]
    c_got_a = swap(c_send_a, "section")
    far, before = ffn_back(grad_1, hidden_0, first, 1)
    before, far, b_far, c_got_a = slot(before, far, b_far, c_got_a)
    ffn_1 = jnp.concatenate([a_keep + a_got, b[0] + b_far])
    direct = lax.axis_size("dp") == 4
    terms = [share(ffn_1, "dp", steps) for steps in range(4)] if direct else []
    some = [shifted(terms[steps], "dp", steps) for steps in (1, 3)] if direct else []
    got = swap(far, "gx")
    c_got_b = swap(c_send_b, "section")
    near, d_hidden, gain_ff = ffn_back(grad_1, hidden_0, first, 0, before)
    near, d_hidden, gain_ff, got, c_got_b, some, terms = slot(
        near, d_hidden, gain_ff, got, c_got_b, some, terms
    )
    some += [shifted(terms[2], "dp", 2)] if direct else []
    a_near, a_far, b = ffn_parts(near, got)
    b_keep, b_send = halves(b, section, 1)
    b_got = swap(b_send, "section")
    a_got = swap(a_far, "gy")
    out_near, out_far, d_q, sent, d_kv = attn_back(
        d_hidden, q_0, mixed_0, kv_0, first, place
    )
    c_1 = [c_keep_1[0] + c_got_a, c_keep_1[1] + c_got_b]
    d_q, sent, some = slot(d_q, sent, some)
    if direct:
        mine_1 = sum((value.astype(F32) for value in some), terms[0].astype(F32)).astype(BF16)
        some = [mine_1, shifted(mine_1, "dp", 1), shifted(mine_1, "dp", 3)]
    behind = to_before(sent)
    query_near, query_far, d_normed = query_back(d_q, normed_0, first)
    query_got, out_got = swap(query_far, "gx"), swap(out_far, "gx")
    d_normed, behind, b_got, a_got, some = slot(d_normed, behind, b_got, a_got, some)
    b = b_keep + b_got
    b_far = swap(b[1], "gy")
    a_keep, a_send = halves(a_near + a_got, section, 0)
    a_got = swap(a_send, "section")
    some += [shifted(some[0], "dp", 2)] if direct else []
    grad_0, d_shared, gain_attn_grad = input_back(
        d_kv, behind, normed_0, d_normed, x, d_hidden, first, place
    )
    grad_0, d_shared, a_got, b_far, some = slot(grad_0, d_shared, a_got, b_far, some)
    ffn_0 = jnp.concatenate([a_keep + a_got, b[0] + b_far])
    if direct:
        ffn_0 = lax.psum(ffn_0, "dp")
        found = jnp.stack([some[0], some[1], some[3], some[2]])
        place = lax.axis_index("dp")
        ffn_1 = jnp.concatenate(
            [
                lax.dynamic_index_in_dim(found, lax.rem(place + 4 - i, 4), 0, keepdims=False)
                for i in range(4)
            ]
        )
    else:
        ffn_1, ffn_0 = lax.psum((ffn_1, ffn_0), "dp")
    near, far = pack_shared(d_shared, gain_attn_grad, gain_ff, order)
    near, got = (query_near, out_near, near), (query_got, out_got, swap(far, "gx"))
    c_keep, c_send = halves(over_cores(near, got), section, 1)
    c_got = swap(c_send, "section")
    c_far_1 = swap(c_1[1], "gy")
    c_keep, c_got, c_far_1, grad_0 = slot(c_keep, c_got, c_far_1, grad_0)
    c = c_keep + c_got
    c_far = swap(c[1], "gy")
    first_rows, second_rows = (jnp.concatenate(rows) for rows in ((out_0, grad_0), (out_1, grad_1)))
    others = swap(pick(section == 0, second_rows, first_rows), "section")
    ffn_0, ffn_1, c_far = slot(ffn_0, ffn_1, c_far)
    attn = jnp.concatenate([c_1[0] + c_far_1, c[0] + c_far])
    sent = pick(section == 0, ffn_1, ffn_0)
    ffn_got = swap(sent, "section")
    attn = lax.psum(attn, "dp")
    states = by_micro(pick(section == 0, out_0, out_1), others[:own_rows])
    in_grads = by_micro(pick(section == 0, grad_0, grad_1), others[own_rows:])
    attn, ffn_got, states, in_grads = slot(attn, ffn_got, states, in_grads)

    def two_halves(one, zero, got):
        mine = pick(section == 0, zero, one)
        return pick(section == 0, mine, got), pick(section == 0, got, mine)

    half = attn.shape[0] // 2
    attn_got = swap(pick(section == 0, attn[:half], attn[half:]), "section")
    ffn_mine = two_halves(ffn_1, ffn_0, ffn_got)
    gate, up, down = finish_ffn(
        ffn_mine, [swap(value, "gx") for value in ffn_mine], gx, scale, w_gate.shape[2]
    )
    attn_got, gate, up, down = slot(attn_got, gate, up, down)
    attn_low, high = two_halves(attn[:half], attn[half:], attn_got)
    attn_others = swap(attn_low, "gx"), swap(high, "gx")
    count = d_shared.shape[0] // STEPS
    quarter = high[-GAIN_ROWS - count : -GAIN_ROWS]
    gain_sums = high[-GAIN_ROWS : 2 - GAIN_ROWS].astype(F32) * scale
    beside = swap(quarter, "gy")
    both = pick(
        gy == 0, jnp.concatenate([quarter, beside]), jnp.concatenate([beside, quarter])
    )
    both_other = swap(both, "gx")
    shared = pick(
        gx == 0, jnp.concatenate([both, both_other]), jnp.concatenate([both_other, both])
    )
    query, key, value, out = finish_attn(
        (attn_low, high), attn_others, shared, gx, scale, w_query.shape[2]
    )

    return (
        states,
        in_grads,
        gain_sums[:1],
        query[None],
        key[None],
        value[None],
        out[None],
        gain_sums[1:],
        gate[None],
        up[None],
        down[None],
    )


def solution(mesh):
    rows = P(None, "dp", ("gx", "gy"), None)
    columns = P("section", None, "gy")
    depth = P("section", "gy", None)
    whole = P("section", None, None)
    gain = P("section", None)
    by_layer = P("section", None, "dp", ("gx", "gy"), None)
    return jax.shard_map(
        local,
        mesh=mesh,
        in_specs=(
            rows,
            P(None, "dp", None),
            rows,
            gain,
            columns,
            whole,
            whole,
            depth,
            gain,
            columns,
            columns,
            depth,
        ),
        out_specs=(
            by_layer,
            by_layer,
            gain,
            columns,
            whole,
            whole,
            depth,
            gain,
            columns,
            columns,
            depth,
        ),
        check_vma=False,
    )
```
